32 devices in a mesh: slab: 2 (over y), ex: 4 (over z), lay: 2 (over x), pb: 2 (over core).
Axes of the slice: x: 2, y: 2, z: 4, core: 2. Of those that a mesh axis runs over, the one named last changes fastest.
Arguments:
- store_grads: bfloat16 [2, 4096, 4096], P('lay', ('slab', 'ex')), parts along dimension 1, may hold values from -0.0625 to 0.0625
- query_grads: bfloat16 [2, 384, 4096], P('lay', ('pb', 'ex')), may hold values from -6 to 6
- query_block: int32 [384], replicated, may hold values from 0 to 3
- layer_slot: int32 [2], replicated, may hold values from 0 to 1, each once
- out_basis: bfloat16 [2, 64, 64], replicated, may hold values from -0.75 to 0.75
- in_basis: bfloat16 [2, 64, 64], replicated, may hold values from -0.75 to 0.75
- eigen_values: float32 [2, 64, 64], replicated, may hold values from 0.05 to 5
- damping: float32 [4], replicated, may hold values from 0.1 to 1
Outputs:
- scores: float32 [4096, 384], P(('slab', 'ex', 'lay'), 'pb'), parts along dimension 0
The draws below stay inside these ranges and needn't reach their ends.
There are 2 independent parts, one for each index of `slab`. The reference program is written for one: setup_inputs(seed, part) draws one part's arguments, and reference() takes and returns one part's arrays. A program takes and returns all parts, laid end to end along the dimension named above; an argument that names none is the same for every part. Nothing has to cross between parts.
Inputs may be any that keep to these rules, and one draw needn't show every extreme that they name: `layer_slot`: a permutation of the 2 model layers.
All inputs are finite; a program needn't handle non-finite values.
Results may differ from the reference program's by a relative error of at most 0.003.
Values may be sent and summed in bfloat16 or wider, within the bound.
No kernel may reach another device: no remote copies, remote signals or barrier semaphores. Data moves between devices by JAX's collectives and lax.ppermute only.
A program may use at most 64 MiB of HBM per device.

```python
import math
import jax
import jax.numpy as jnp
from jax import lax

OUT_RANK = 64
IN_RANK = 64
DIM = 4096
BLOCKS = 4
LAYERS = 2
EXAMPLES = 2048
QUERIES = 384


def with_ends(drawn, key, smallest, high):
    spot = [jax.random.randint(jax.random.fold_in(key, axis), (), 0, length) for axis, length in enumerate(drawn.shape)]
    widest = drawn.shape.index(max(drawn.shape))
    next_to = spot[:widest] + [(spot[widest] + 1) % drawn.shape[widest]] + spot[widest + 1:]
    return drawn.at[tuple(spot)].set(smallest).at[tuple(next_to)].set(high)


def block_scale(stream_key, dims, cuts, low, largest):
    level = 1.0
    for position, shards_of in cuts:
        heights = jax.random.uniform(jax.random.fold_in(jax.random.fold_in(stream_key, 6), position), (shards_of,), jnp.float32, low / len(cuts), largest / len(cuts))
        level = level * jnp.repeat(jnp.exp(heights), dims[position] // shards_of).reshape((-1,) + (1,) * (len(dims) - 1 - position))
    return level


def centred(key, dims, width, limit, shards=(), kind=jnp.bfloat16):
    values = jax.random.normal(key, dims, jnp.float32) * width
    if len(shards) > 0:
        values = block_scale(key, dims, shards, -0.22, 0.18) * values
    return jnp.clip(values, min=-limit, max=limit).astype(kind)


def setup_inputs(seed: int = 0, part: int = 0) -> dict:
    splits = jax.random.split(jax.random.key(seed), 9)
    part_keys = jax.random.split(jax.random.fold_in(splits[8], part), 9)
    store_grads = centred(part_keys[0], (LAYERS, EXAMPLES, DIM), (DIM * LAYERS) ** -0.5, 0.0625, ((0, 2), (1, 4)))
    query_grads = centred(splits[1], (LAYERS, QUERIES, DIM), 1.0, 6.0, ((0, 2), (1, 8)))
    query_block = with_ends(jax.random.randint(splits[2], (QUERIES,), 0, BLOCKS), jax.random.fold_in(splits[2], 1), 0, BLOCKS - 1).astype(jnp.int32)
    layer_slot = jax.random.permutation(splits[3], LAYERS).astype(jnp.int32)
    out_basis = centred(splits[4], (LAYERS, OUT_RANK, OUT_RANK), OUT_RANK ** -0.5, 0.75)
    in_basis = centred(splits[5], (LAYERS, IN_RANK, IN_RANK), IN_RANK ** -0.5, 0.75)
    eigen_values = jnp.clip(jnp.exp(jax.random.uniform(splits[6], (LAYERS, OUT_RANK, IN_RANK), jnp.float32, math.log(0.05), math.log(5.0))), 0.05, 5.0)
    damping = jnp.clip(jnp.exp(jax.random.uniform(splits[7], (BLOCKS,), jnp.float32, math.log(0.1), math.log(1.0))), 0.1, 1.0)
    return {"store_grads": store_grads, "query_grads": query_grads, "query_block": query_block, "layer_slot": layer_slot, "out_basis": out_basis, "in_basis": in_basis, "eigen_values": eigen_values, "damping": damping}


HIGHEST = lax.Precision.HIGHEST


def lookup_damping(block_ids, damping):
    hits = block_ids[:, None] == jnp.arange(BLOCKS, dtype=jnp.int32)[None, :]
    return jnp.sum(jnp.where(hits, damping[None, :], jnp.float32(0.0)), axis=1)


def rotate(block_rows, out_factor, in_factor, eigen_layer, damp_rows):
    count_rows = block_rows.shape[0]
    grid_rows = block_rows.astype(jnp.float32).reshape(count_rows, OUT_RANK, IN_RANK)
    left_side = jnp.einsum("ap,nai->npi", out_factor, grid_rows, precision=HIGHEST)
    middle = jnp.einsum("npi,iq->npq", left_side, in_factor, precision=HIGHEST)
    scaled = middle / (eigen_layer[None] + damp_rows[:, None, None])
    turned = jnp.einsum("ap,npq->naq", out_factor, scaled, precision=HIGHEST)
    result = jnp.einsum("naq,bq->nab", turned, in_factor, precision=HIGHEST)
    return result.reshape(count_rows, OUT_RANK * IN_RANK).astype(jnp.bfloat16)


def reference(store_grads, query_grads, query_block, layer_slot, out_basis, in_basis, eigen_values, damping):
    damp_rows = lookup_damping(query_block, damping)
    scores = jnp.zeros((EXAMPLES, QUERIES), jnp.float32)
    for slot in range(LAYERS):
        model_layer = layer_slot[slot]
        rotated = rotate(query_grads[slot], out_basis[model_layer].astype(jnp.float32),
                         in_basis[model_layer].astype(jnp.float32), eigen_values[model_layer], damp_rows)
        scores = scores + jnp.dot(store_grads[slot], rotated.T, preferred_element_type=jnp.float32)
    return scores
```

```python
import functools

import jax
import jax.numpy as jnp
from jax import lax
from jax.experimental import pallas as pl
from jax.experimental.pallas import tpu as pltpu
from jax.sharding import PartitionSpec as P

RANK = 64
BLOCKS = 4
F32 = jnp.float32
BF16 = jnp.bfloat16
NT = (((1,), (1,)), ((), ()))
RING = ("slab", "ex")


def split(x):
    hi = x.astype(BF16)
    return hi, (x - hi.astype(F32)).astype(BF16)


def rotate_kernel(
    half, lay_slots, block_ref, damping_ref, slot_ref, query_ref, out_ref, in_ref, eigen_ref,
    result_ref, rows_ref, basis_ref, turned_ref,
):
    pairs = RANK * RANK // 128
    local = query_ref.shape[1]
    slab = lax.axis_index("slab")
    first = (lax.axis_index("pb") * lax.axis_size("ex") + lax.axis_index("ex")) * local + slab * half
    model_layer = slot_ref[lax.axis_index("lay") * lay_slots]
    low_lanes = lax.broadcasted_iota(jnp.int32, (RANK // 2, 128), 1) < RANK

    for pair in range(pairs):
        block = query_ref[0, :, pair * 128:(pair + 1) * 128].astype(F32)
        rows_ref[pair * half:(pair + 1) * half, :] = jnp.where(slab == 0, block[:half], block[half:2 * half])

    basis_ref[:, :RANK] = out_ref[model_layer].astype(F32)
    out_rows = jnp.concatenate(
        [basis_ref[pl.ds(0, RANK // 2, stride=2), :], basis_ref[pl.ds(1, RANK // 2, stride=2), :]], axis=0
    )
    out_t = out_rows.T[:RANK].astype(BF16)
    out_rows = out_rows[:, :RANK].astype(BF16)
    out_twice = jnp.concatenate([out_rows, out_rows], axis=1)
    out_t_twice = jnp.concatenate([out_t, out_t], axis=1)

    in_wide = jnp.concatenate([in_ref[model_layer].astype(F32)] * 4, axis=1)
    in_tall = jnp.concatenate([in_wide] * 4, axis=0)
    row = lax.broadcasted_iota(jnp.int32, in_tall.shape, 0) // RANK
    col = lax.broadcasted_iota(jnp.int32, in_tall.shape, 1) // RANK
    in_diag = jnp.where(row == col, in_tall, F32(0.0)).astype(BF16)

    eigen = jnp.concatenate([eigen_ref[model_layer]] * 4, axis=1)
    lane = lax.broadcasted_iota(jnp.int32, (1, 4 * RANK), 1) // RANK

    for quad in range(half // 4):
        tops, bottoms = [], []
        for two in range(2):
            at = quad * 4 + two * 2
            a = rows_ref[pl.ds(at, pairs, stride=half), :]
            b = rows_ref[pl.ds(at + 1, pairs, stride=half), :]
            tops.append(jnp.where(low_lanes, a, pltpu.roll(b, RANK, 1)))
            bottoms.append(jnp.where(low_lanes, pltpu.roll(a, RANK, 1), b))
        grid = jnp.concatenate(
            [jnp.concatenate(tops, axis=1), jnp.concatenate(bottoms, axis=1)], axis=0
        ).astype(BF16)
        right = jnp.dot(grid, in_diag, preferred_element_type=F32)
        middle = jnp.dot(out_t_twice, jnp.concatenate(split(right), axis=0), preferred_element_type=F32)
        damp = jnp.zeros((1, 4 * RANK), F32)
        for one in range(4):
            block = block_ref[first + quad * 4 + one]
            value = F32(0.0)
            for k in range(BLOCKS):
                value = jnp.where(block == k, damping_ref[k], value)
            damp = jnp.where(lane == one, value, damp)
        scaled = middle / (eigen + damp)
        turned = jnp.dot(out_twice, jnp.concatenate(split(scaled), axis=0), preferred_element_type=F32)
        hi, lo = split(turned)
        result = lax.dot_general(hi, in_diag, NT, preferred_element_type=F32)
        result = result + lax.dot_general(lo, in_diag, NT, preferred_element_type=F32)
        for two in range(2):
            at = quad * 4 + two * 2
            top = result[:pairs, two * 128:(two + 1) * 128]
            bottom = result[pairs:, two * 128:(two + 1) * 128]
            turned_ref[pl.ds(at, pairs, stride=half), :] = jnp.where(low_lanes, top, pltpu.roll(bottom, RANK, 1))
            turned_ref[pl.ds(at + 1, pairs, stride=half), :] = jnp.where(low_lanes, pltpu.roll(top, RANK, 1), bottom)

    for pair in range(pairs):
        result_ref[:, pair * 128:(pair + 1) * 128] = turned_ref[pair * half:(pair + 1) * half, :].astype(BF16)


def rotate(query_grads, query_block, layer_slot, out_basis, in_basis, eigen_values, damping):
    half = query_grads.shape[1] // lax.axis_size("slab")
    dim = query_grads.shape[2]
    vmem = pl.BlockSpec(memory_space=pltpu.VMEM)
    smem = pl.BlockSpec(memory_space=pltpu.SMEM)
    return pl.pallas_call(
        functools.partial(rotate_kernel, half, 1),
        out_shape=jax.ShapeDtypeStruct((half, dim), BF16),
        in_specs=[smem, smem, smem, vmem, vmem, vmem, vmem],
        out_specs=vmem,
        scratch_shapes=[
            pltpu.VMEM((half * dim // 128, 128), F32),
            pltpu.VMEM((RANK, 128), F32),
            pltpu.VMEM((half * dim // 128, 128), F32),
        ],
        compiler_params=pltpu.CompilerParams(vmem_limit_bytes=16 << 20),
        cost_estimate=pl.CostEstimate(flops=8 * half * dim * 256, bytes_accessed=1 << 20, transcendentals=0),
        name="rotate",
    )(query_block, damping, layer_slot, query_grads, out_basis, in_basis, eigen_values)


def score_kernel(count, height, share, shares, *refs):
    pieces, store_ref = refs[:count], refs[count]
    keep_ref, sends, held = refs[count + 1], refs[count + 2:-1], refs[-1]
    half, width = pieces[0].shape
    dim = store_ref.shape[2]
    if width == dim:
        for k, piece in enumerate(pieces):
            held[k * height:k * height + half, :] = piece[...]
        whole = count
    else:
        for k, piece in enumerate(pieces):
            held[:half, k * width:(k + 1) * width] = piece[...]
        whole = 1
    lay = lax.axis_index("lay")
    for k in range(shares):
        owner = lax.rem(lay + k, shares)
        rows = pl.ds(pl.multiple_of(owner * share, share), share)
        block = lax.dot_general(held[...], store_ref[0, rows, :], NT, preferred_element_type=F32)
        target = keep_ref if k == 0 else sends[k - 1]
        for j in range(whole):
            target[j * half:(j + 1) * half, :] = block[j * height:j * height + half].astype(target.dtype)


def score(pieces, store):
    half, width = pieces[0].shape
    _, examples, dim = store.shape
    shares = lax.axis_size("lay")
    share = examples // shares
    whole = len(pieces) if width == dim else 1
    height = -(-half // 16) * 16
    vmem = pl.BlockSpec(memory_space=pltpu.VMEM)
    shape = (whole * half, share)
    out = pl.pallas_call(
        functools.partial(score_kernel, len(pieces), height, share, shares),
        out_shape=[jax.ShapeDtypeStruct(shape, F32)] + [jax.ShapeDtypeStruct(shape, BF16)] * (shares - 1),
        in_specs=[vmem] * (len(pieces) + 1),
        out_specs=[vmem] * shares,
        scratch_shapes=[pltpu.VMEM((whole * height, dim), BF16)],
        compiler_params=pltpu.CompilerParams(vmem_limit_bytes=24 << 20),
        cost_estimate=pl.CostEstimate(flops=2 * 256 * examples * dim, bytes_accessed=1 << 20, transcendentals=0),
        name="score",
    )(*pieces, store)
    return out[0], out[1:]


def swap_layers(sends):
    shares = lax.axis_size("lay")
    return [
        lax.ppermute(send, "lay", [(i, (i + k + 1) % shares) for i in range(shares)])
        for k, send in enumerate(sends)
    ]


def finish_kernel(half, members, sizes, *refs):
    out_ref = refs[-1]
    refs = refs[:-1]
    count = len(sizes)
    each = len(refs) // count
    slab, ex = lax.axis_index("slab"), lax.axis_index("ex")
    place = jnp.where(slab == 0, ex, 2 * members - 1 - ex)
    step = jnp.where(lax.rem(place, 2) == 0, 1, 2 * members - 1)
    at = 0
    for k, size in enumerate(sizes):
        keep, got = refs[k * each], refs[k * each + 1:(k + 1) * each]
        for j in range(size):
            rows = slice(j * half, (j + 1) * half)
            total = keep[rows, :]
            for g in got:
                total = total + g[rows, :].astype(F32)
            distance, side = (at + 1) // 2, (at + 1) % 2
            hops = distance if side == 0 else 2 * members - distance
            source = lax.rem(place + hops * step, 2 * members)
            block = jnp.where(source < members, 2 * source, 2 * (2 * members - 1 - source) + 1)
            out_ref[pl.ds(pl.multiple_of(block * half, 8), half), :] = total
            at += 1


def finish(half, parts):
    members = lax.axis_size("ex")
    vmem = pl.BlockSpec(memory_space=pltpu.VMEM)
    flat = [array for keep, got in parts for array in [keep, *got]]
    sizes = [keep.shape[0] // half for keep, _ in parts]
    return pl.pallas_call(
        functools.partial(finish_kernel, half, members, sizes),
        out_shape=jax.ShapeDtypeStruct((2 * members * half, flat[0].shape[1]), F32),
        in_specs=[vmem] * len(flat),
        out_specs=vmem,
        compiler_params=pltpu.CompilerParams(vmem_limit_bytes=16 << 20),
        name="finish",
    )(*flat)


def local(
    store_grads, query_grads, query_block, layer_slot, out_basis, in_basis, eigen_values, damping
):
    members = lax.axis_size("ex")
    ring = list(range(members)) + [members + i for i in reversed(range(members))]
    edges = [[], []]
    for i, a in enumerate(ring):
        b = ring[(i + 1) % len(ring)]
        edges[i % 2] += [(a, b), (b, a)]
    own = rotate(query_grads, query_block, layer_slot, out_basis, in_basis, eigen_values, damping)
    half, dim = own.shape
    even = odd = own
    batch, parts = [own], []
    for step in range(1, members + 1):
        if step == members:
            even, odd = even[:, dim // 2:], odd[:, :dim // 2]
        even, odd = lax.ppermute(odd, RING, edges[0]), lax.ppermute(even, RING, edges[1])
        if step < members:
            batch += [even, odd]
        if len(batch) >= 5 or step >= members - 1:
            if step == members:
                batch = [even, odd]
            keep, sends = score(batch, store_grads)
            parts.append((keep, swap_layers(sends)))
            batch = []
    return finish(half, parts).T


def solution(mesh):
    return jax.shard_map(
        local,
        mesh=mesh,
        in_specs=(
            P("lay", ("slab", "ex"), None),
            P("lay", ("pb", "ex"), None),
            P(),
            P(),
            P(),
            P(),
            P(),
            P(),
        ),
        out_specs=P(("slab", "ex", "lay"), "pb"),
        check_vma=False,
    )
```

```python
import functools

import jax
import jax.numpy as jnp
from jax import lax
from jax.experimental import pallas as pl
from jax.experimental.pallas import tpu as pltpu
from jax.sharding import PartitionSpec as P

RANK = 64
BLOCKS = 4
F32 = jnp.float32
BF16 = jnp.bfloat16
NT = (((1,), (1,)), ((), ()))
RING = ("slab", "ex")


def in_hbm(x):
    return pltpu.with_memory_space_constraint(x, pltpu.HBM)


def split(x):
    hi = x.astype(BF16)
    return hi, (x - hi.astype(F32)).astype(BF16)


def rotate_kernel(
    half, lay_slots, query_hbm, block_hbm, damping_hbm, slot_hbm, out_hbm, in_hbm, eigen_hbm,
    result_ref, query_ref, block_ref, damping_ref, slot_ref, out_ref, in_ref, eigen_ref,
    rows_ref, basis_ref, turned_ref, sems,
):
    pairs = RANK * RANK // 128
    local = query_ref.shape[1]
    copies = [
        pltpu.make_async_copy(source, target, sems.at[k])
        for k, (source, target) in enumerate([
            (slot_hbm, slot_ref), (query_hbm, query_ref), (block_hbm, block_ref), (damping_hbm, damping_ref),
            (out_hbm, out_ref), (in_hbm, in_ref), (eigen_hbm, eigen_ref),
        ])
    ]
    for copy in copies:
        copy.start()
    slab = lax.axis_index("slab")
    first = (lax.axis_index("pb") * lax.axis_size("ex") + lax.axis_index("ex")) * local + slab * half
    low_lanes = lax.broadcasted_iota(jnp.int32, (RANK // 2, 128), 1) < RANK
    row = lax.broadcasted_iota(jnp.int32, (4 * RANK, 4 * RANK), 0) // RANK
    col = lax.broadcasted_iota(jnp.int32, (4 * RANK, 4 * RANK), 1) // RANK
    lane = lax.broadcasted_iota(jnp.int32, (1, 4 * RANK), 1) // RANK
    for copy in copies:
        copy.wait()
    model_layer = slot_ref[lax.axis_index("lay") * lay_slots]

    for pair in range(pairs):
        block = query_ref[0, :, pair * 128:(pair + 1) * 128].astype(F32)
        rows_ref[pair * half:(pair + 1) * half, :] = jnp.where(slab == 0, block[:half], block[half:2 * half])

    basis_ref[:, :RANK] = out_ref[model_layer].astype(F32)
    out_rows = jnp.concatenate(
        [basis_ref[pl.ds(0, RANK // 2, stride=2), :], basis_ref[pl.ds(1, RANK // 2, stride=2), :]], axis=0
    )
    out_t = out_rows.T[:RANK].astype(BF16)
    out_rows = out_rows[:, :RANK].astype(BF16)
    out_twice = jnp.concatenate([out_rows, out_rows], axis=1)
    out_t_twice = jnp.concatenate([out_t, out_t], axis=1)

    in_wide = jnp.concatenate([in_ref[model_layer].astype(F32)] * 4, axis=1)
    in_tall = jnp.concatenate([in_wide] * 4, axis=0)
    in_diag = jnp.where(row == col, in_tall, F32(0.0)).astype(BF16)
    eigen = jnp.concatenate([eigen_ref[model_layer]] * 4, axis=1)

    quads = range(half // 4)
    grids = []
    for quad in quads:
        tops, bottoms = [], []
        for two in range(2):
            at = quad * 4 + two * 2
            a = rows_ref[pl.ds(at, pairs, stride=half), :]
            b = rows_ref[pl.ds(at + 1, pairs, stride=half), :]
            tops.append(jnp.where(low_lanes, a, pltpu.roll(b, RANK, 1)))
            bottoms.append(jnp.where(low_lanes, pltpu.roll(a, RANK, 1), b))
        grids += [jnp.concatenate(tops, axis=1), jnp.concatenate(bottoms, axis=1)]
    right = jnp.dot(jnp.concatenate(grids, axis=0).astype(BF16), in_diag, preferred_element_type=F32)
    turned = []
    for quad in quads:
        part = right[quad * RANK:(quad + 1) * RANK]
        middle = jnp.dot(out_t_twice, jnp.concatenate(split(part), axis=0), preferred_element_type=F32)
        damp = jnp.zeros((1, 4 * RANK), F32)
        for one in range(4):
            block = block_ref[first + quad * 4 + one]
            value = F32(0.0)
            for k in range(BLOCKS):
                value = jnp.where(block == k, damping_ref[k], value)
            damp = jnp.where(lane == one, value, damp)
        scaled = middle / (eigen + damp)
        turned.append(jnp.dot(out_twice, jnp.concatenate(split(scaled), axis=0), preferred_element_type=F32))
    hi, lo = split(jnp.concatenate(turned, axis=0))
    result = lax.dot_general(hi, in_diag, NT, preferred_element_type=F32)
    result = result + lax.dot_general(lo, in_diag, NT, preferred_element_type=F32)
    for quad in quads:
        for two in range(2):
            at = quad * 4 + two * 2
            top = result[quad * RANK:quad * RANK + pairs, two * 128:(two + 1) * 128]
            bottom = result[quad * RANK + pairs:(quad + 1) * RANK, two * 128:(two + 1) * 128]
            turned_ref[pl.ds(at, pairs, stride=half), :] = jnp.where(low_lanes, top, pltpu.roll(bottom, RANK, 1))
            turned_ref[pl.ds(at + 1, pairs, stride=half), :] = jnp.where(low_lanes, pltpu.roll(top, RANK, 1), bottom)

    for pair in range(pairs):
        result_ref[:, pair * 128:(pair + 1) * 128] = turned_ref[pair * half:(pair + 1) * half, :].astype(BF16)


def rotate(query_grads, query_block, layer_slot, out_basis, in_basis, eigen_values, damping):
    half = query_grads.shape[1] // lax.axis_size("slab")
    dim = query_grads.shape[2]
    operands = (query_grads, query_block, damping, layer_slot, out_basis, in_basis, eigen_values)
    homes = (pltpu.VMEM, pltpu.SMEM, pltpu.SMEM, pltpu.SMEM, pltpu.VMEM, pltpu.VMEM, pltpu.VMEM)
    return pl.pallas_call(
        functools.partial(rotate_kernel, half, 1),
        out_shape=jax.ShapeDtypeStruct((half, dim), BF16),
        in_specs=[pl.BlockSpec(memory_space=pltpu.HBM)] * len(operands),
        out_specs=pl.BlockSpec(memory_space=pltpu.VMEM),
        scratch_shapes=[home(x.shape, x.dtype) for home, x in zip(homes, operands)] + [
            pltpu.VMEM((half * dim // 128, 128), F32),
            pltpu.VMEM((RANK, 128), F32),
            pltpu.VMEM((half * dim // 128, 128), F32),
            pltpu.SemaphoreType.DMA((len(operands),)),
        ],
        compiler_params=pltpu.CompilerParams(vmem_limit_bytes=16 << 20),
        cost_estimate=pl.CostEstimate(flops=8 * half * dim * 256, bytes_accessed=1 << 20, transcendentals=0),
        name="rotate",
    )(*map(in_hbm, operands))


def fetch_kernel(after_ref, store_hbm, store_ref, sems):
    del after_ref
    parts = sems.shape[0]
    rows = store_ref.shape[1] // parts
    copies = [
        pltpu.make_async_copy(
            store_hbm.at[:, pl.ds(k * rows, rows)], store_ref.at[:, pl.ds(k * rows, rows)], sems.at[k]
        )
        for k in range(parts)
    ]
    for copy in copies:
        copy.start()
    for copy in copies:
        copy.wait()


def fetch(after, store):
    return pl.pallas_call(
        fetch_kernel,
        out_shape=jax.ShapeDtypeStruct(store.shape, store.dtype),
        in_specs=[pl.BlockSpec(memory_space=pltpu.VMEM), pl.BlockSpec(memory_space=pltpu.HBM)],
        out_specs=pl.BlockSpec(memory_space=pltpu.VMEM),
        scratch_shapes=[pltpu.SemaphoreType.DMA((4,))],
        compiler_params=pltpu.CompilerParams(vmem_limit_bytes=8 << 20),
        cost_estimate=pl.CostEstimate(flops=0, bytes_accessed=2 * store.size * 2, transcendentals=0),
        name="fetch",
    )(after, in_hbm(store))


def score_kernel(count, height, share, shares, owners, *refs):
    outs, held = refs[-1 - len(owners):-1], refs[-1]
    pieces, store_ref = refs[:-2 - len(owners)], refs[-2 - len(owners)]
    half = pieces[0].shape[0]
    for k, piece in enumerate(pieces[:count]):
        held[k * height:k * height + half, :] = piece[...]
    for k, piece in enumerate(pieces[count:]):
        width = piece.shape[1]
        held[count * height:count * height + half, k * width:(k + 1) * width] = piece[...]
    lay = lax.axis_index("lay")
    for out, owner in zip(outs, owners):
        rows = pl.ds(pl.multiple_of(lax.rem(lay + owner, shares) * share, share), share)
        block = lax.dot_general(held[...], store_ref[0, rows, :], NT, preferred_element_type=F32)
        for j in range(out.shape[0] // half):
            out[j * half:(j + 1) * half, :] = block[j * height:j * height + half].astype(out.dtype)


def score(pieces, parts, store, owners):
    half = (pieces + parts)[0].shape[0]
    _, examples, dim = store.shape
    shares = lax.axis_size("lay")
    share = examples // shares
    whole = len(pieces) + (1 if parts else 0)
    height = -(-half // 16) * 16
    vmem = pl.BlockSpec(memory_space=pltpu.VMEM)
    return pl.pallas_call(
        functools.partial(score_kernel, len(pieces), height, share, shares, tuple(owners)),
        out_shape=[jax.ShapeDtypeStruct((whole * half, share), BF16 if owner else F32) for owner in owners],
        in_specs=[vmem] * (len(pieces) + len(parts) + 1),
        out_specs=[vmem] * len(owners),
        scratch_shapes=[pltpu.VMEM((whole * height, dim), BF16)],
        compiler_params=pltpu.CompilerParams(vmem_limit_bytes=24 << 20),
        cost_estimate=pl.CostEstimate(
            flops=2 * 256 * share * len(owners) * dim, bytes_accessed=1 << 20, transcendentals=0
        ),
        name="score",
    )(*pieces, *parts, store)


def swap_layers(sends):
    shares = lax.axis_size("lay")
    return [
        lax.ppermute(send, "lay", [(i, (i + k + 1) % shares) for i in range(shares)])
        for k, send in enumerate(sends)
    ]


def finish_kernel(half, members, sizes, *refs):
    out_ref = refs[-1]
    refs = refs[:-1]
    count = len(sizes)
    each = len(refs) // count
    slab, ex = lax.axis_index("slab"), lax.axis_index("ex")
    place = jnp.where(slab == 0, ex, 2 * members - 1 - ex)
    at = 0
    for k, size in enumerate(sizes):
        keep, got = refs[k * each], refs[k * each + 1:(k + 1) * each]
        for j in range(size):
            rows = slice(j * half, (j + 1) * half)
            total = keep[rows, :]
            for g in got:
                total = total + g[rows, :].astype(F32)
            distance = (at + 1) // 2
            hops = 2 * members - distance if at % 2 == 1 else distance
            source = lax.rem(place + hops, 2 * members)
            block = jnp.where(source < members, 2 * source, 2 * (2 * members - 1 - source) + 1)
            out_ref[pl.ds(pl.multiple_of(block * half, 8), half), :] = total
            at += 1


def finish(half, parts):
    members = lax.axis_size("ex")
    vmem = pl.BlockSpec(memory_space=pltpu.VMEM)
    flat = [array for keep, got in parts for array in [keep, *got]]
    sizes = [keep.shape[0] // half for keep, _ in parts]
    return pl.pallas_call(
        functools.partial(finish_kernel, half, members, sizes),
        out_shape=jax.ShapeDtypeStruct((2 * members * half, flat[0].shape[1]), F32),
        in_specs=[vmem] * len(flat),
        out_specs=vmem,
        compiler_params=pltpu.CompilerParams(vmem_limit_bytes=16 << 20),
        name="finish",
    )(*flat)


def local(
    store_grads, query_grads, query_block, layer_slot, out_basis, in_basis, eigen_values, damping
):
    members = lax.axis_size("ex")
    ring = list(range(members)) + [members + i for i in reversed(range(members))]
    forth = [(a, ring[(i + 1) % len(ring)]) for i, a in enumerate(ring)]
    back = [(b, a) for a, b in forth]
    own = rotate(query_grads, query_block, layer_slot, out_basis, in_basis, eigen_values, damping)
    store = fetch(own, store_grads)
    half, dim = own.shape
    others = range(1, lax.axis_size("lay"))
    one = two = own
    batch, sums, hidden = [own], [], store
    for step in range(1, members):
        one, two = lax.ppermute(one, RING, forth), lax.ppermute(two, RING, back)
        one, two, hidden = lax.optimization_barrier((one, two, hidden))
        if step == 1:
            store = hidden
        elif hidden:
            sums.append((keep, swap_layers(hidden)))
        hidden = []
        batch += [one, two]
        if len(batch) >= 5 and step < members - 1:
            keep, *hidden = score(batch, [], store, [0, *others])
            batch = []
    parts = [lax.ppermute(one[:, :dim // 2], RING, forth), lax.ppermute(two[:, dim // 2:], RING, back)]
    got = swap_layers(score(batch, parts, store, others))
    sums.append((*score(batch, parts, store, [0]), got))
    return finish(half, sums).T


def solution(mesh):
    return jax.shard_map(
        local,
        mesh=mesh,
        in_specs=(
            P("lay", ("slab", "ex"), None),
            P("lay", ("pb", "ex"), None),
            P(),
            P(),
            P(),
            P(),
            P(),
            P(),
        ),
        out_specs=P(("slab", "ex", "lay"), "pb"),
        check_vma=False,
    )
```

```python
import functools

import jax
import jax.numpy as jnp
from jax import lax
from jax.experimental import pallas as pl
from jax.experimental.pallas import tpu as pltpu
from jax.sharding import PartitionSpec as P

RANK = 64
BLOCKS = 4
F32 = jnp.float32
BF16 = jnp.bfloat16
NT = (((1,), (1,)), ((), ()))
RING = ("slab", "ex")


def in_hbm(x):
    return pltpu.with_memory_space_constraint(x, pltpu.HBM)


def split(x):
    hi = x.astype(BF16)
    return hi, (x - hi.astype(F32)).astype(BF16)


def rotate_kernel(
    half, lay_slots, query_hbm, block_hbm, damping_hbm, slot_hbm, out_hbm, in_hbm, eigen_hbm, store_hbm,
    result_ref, store_ref, query_ref, block_ref, damping_ref, slot_ref, out_ref, in_ref, eigen_ref,
    rows_ref, basis_ref, turned_ref, sems, store_sems,
):
    pairs = RANK * RANK // 128
    local = query_ref.shape[1]
    copies = [
        pltpu.make_async_copy(source, target, sems.at[k])
        for k, (source, target) in enumerate([
            (slot_hbm, slot_ref), (query_hbm, query_ref), (block_hbm, block_ref), (damping_hbm, damping_ref),
            (out_hbm, out_ref), (in_hbm, in_ref), (eigen_hbm, eigen_ref),
        ])
    ]
    stretch = store_ref.shape[1] // store_sems.shape[0]
    store_copies = [
        pltpu.make_async_copy(
            store_hbm.at[:, pl.ds(k * stretch, stretch)], store_ref.at[:, pl.ds(k * stretch, stretch)], store_sems.at[k]
        )
        for k in range(store_sems.shape[0])
    ]
    for copy in copies + store_copies:
        copy.start()
    slab = lax.axis_index("slab")
    first = (lax.axis_index("pb") * lax.axis_size("ex") + lax.axis_index("ex")) * local + slab * half
    low_lanes = lax.broadcasted_iota(jnp.int32, (RANK // 2, 128), 1) < RANK
    row = lax.broadcasted_iota(jnp.int32, (4 * RANK, 4 * RANK), 0) // RANK
    col = lax.broadcasted_iota(jnp.int32, (4 * RANK, 4 * RANK), 1) // RANK
    lane = lax.broadcasted_iota(jnp.int32, (1, 4 * RANK), 1) // RANK
    for copy in copies:
        copy.wait()
    model_layer = slot_ref[lax.axis_index("lay") * lay_slots]

    for pair in range(pairs):
        block = query_ref[0, :, pair * 128:(pair + 1) * 128].astype(F32)
        rows_ref[pair * half:(pair + 1) * half, :] = jnp.where(slab == 0, block[:half], block[half:2 * half])

    basis_ref[:, :RANK] = out_ref[model_layer].astype(F32)
    out_rows = jnp.concatenate(
        [basis_ref[pl.ds(0, RANK // 2, stride=2), :], basis_ref[pl.ds(1, RANK // 2, stride=2), :]], axis=0
    )
    out_t = out_rows.T[:RANK].astype(BF16)
    out_rows = out_rows[:, :RANK].astype(BF16)
    out_twice = jnp.concatenate([out_rows, out_rows], axis=1)
    out_t_twice = jnp.concatenate([out_t, out_t], axis=1)

    in_wide = jnp.concatenate([in_ref[model_layer].astype(F32)] * 4, axis=1)
    in_tall = jnp.concatenate([in_wide] * 4, axis=0)
    in_diag = jnp.where(row == col, in_tall, F32(0.0)).astype(BF16)
    eigen = jnp.concatenate([eigen_ref[model_layer]] * 4, axis=1)

    quads = range(half // 4)
    grids = []
    for quad in quads:
        tops, bottoms = [], []
        for two in range(2):
            at = quad * 4 + two * 2
            a = rows_ref[pl.ds(at, pairs, stride=half), :]
            b = rows_ref[pl.ds(at + 1, pairs, stride=half), :]
            tops.append(jnp.where(low_lanes, a, pltpu.roll(b, RANK, 1)))
            bottoms.append(jnp.where(low_lanes, pltpu.roll(a, RANK, 1), b))
        grids += [jnp.concatenate(tops, axis=1), jnp.concatenate(bottoms, axis=1)]
    right = jnp.dot(jnp.concatenate(grids, axis=0).astype(BF16), in_diag, preferred_element_type=F32)
    turned = []
    for quad in quads:
        part = right[quad * RANK:(quad + 1) * RANK]
        middle = jnp.dot(out_t_twice, jnp.concatenate(split(part), axis=0), preferred_element_type=F32)
        damp = jnp.zeros((1, 4 * RANK), F32)
        for one in range(4):
            block = block_ref[first + quad * 4 + one]
            value = F32(0.0)
            for k in range(BLOCKS):
                value = jnp.where(block == k, damping_ref[k], value)
            damp = jnp.where(lane == one, value, damp)
        scaled = middle / (eigen + damp)
        turned.append(jnp.dot(out_twice, jnp.concatenate(split(scaled), axis=0), preferred_element_type=F32))
    hi, lo = split(jnp.concatenate(turned, axis=0))
    result = lax.dot_general(hi, in_diag, NT, preferred_element_type=F32)
    result = result + lax.dot_general(lo, in_diag, NT, preferred_element_type=F32)
    for quad in quads:
        for two in range(2):
            at = quad * 4 + two * 2
            top = result[quad * RANK:quad * RANK + pairs, two * 128:(two + 1) * 128]
            bottom = result[quad * RANK + pairs:(quad + 1) * RANK, two * 128:(two + 1) * 128]
            turned_ref[pl.ds(at, pairs, stride=half), :] = jnp.where(low_lanes, top, pltpu.roll(bottom, RANK, 1))
            turned_ref[pl.ds(at + 1, pairs, stride=half), :] = jnp.where(low_lanes, pltpu.roll(top, RANK, 1), bottom)

    for pair in range(pairs):
        result_ref[:, pair * 128:(pair + 1) * 128] = turned_ref[pair * half:(pair + 1) * half, :].astype(BF16)
    for copy in store_copies:
        copy.wait()


def rotate(query_grads, query_block, layer_slot, out_basis, in_basis, eigen_values, damping, store):
    half = query_grads.shape[1] // lax.axis_size("slab")
    dim = query_grads.shape[2]
    operands = (query_grads, query_block, damping, layer_slot, out_basis, in_basis, eigen_values)
    homes = (pltpu.VMEM, pltpu.SMEM, pltpu.SMEM, pltpu.SMEM, pltpu.VMEM, pltpu.VMEM, pltpu.VMEM)
    return pl.pallas_call(
        functools.partial(rotate_kernel, half, 1),
        out_shape=[jax.ShapeDtypeStruct((half, dim), BF16), jax.ShapeDtypeStruct(store.shape, store.dtype)],
        in_specs=[pl.BlockSpec(memory_space=pltpu.HBM)] * (len(operands) + 1),
        out_specs=[pl.BlockSpec(memory_space=pltpu.VMEM)] * 2,
        scratch_shapes=[home(x.shape, x.dtype) for home, x in zip(homes, operands)] + [
            pltpu.VMEM((half * dim // 128, 128), F32),
            pltpu.VMEM((RANK, 128), F32),
            pltpu.VMEM((half * dim // 128, 128), F32),
            pltpu.SemaphoreType.DMA((len(operands),)),
            pltpu.SemaphoreType.DMA((4,)),
        ],
        compiler_params=pltpu.CompilerParams(vmem_limit_bytes=16 << 20),
        cost_estimate=pl.CostEstimate(flops=8 * half * dim * 256, bytes_accessed=1 << 20, transcendentals=0),
        name="rotate",
    )(*map(in_hbm, operands), in_hbm(store))


def score_kernel(count, height, share, shares, owners, *refs):
    outs, held = refs[-1 - len(owners):-1], refs[-1]
    pieces, store_ref = refs[:-2 - len(owners)], refs[-2 - len(owners)]
    half = pieces[0].shape[0]
    for k, piece in enumerate(pieces[:count]):
        held[k * height:k * height + half, :] = piece[...]
    for k, piece in enumerate(pieces[count:]):
        width = piece.shape[1]
        held[count * height:count * height + half, k * width:(k + 1) * width] = piece[...]
    lay = lax.axis_index("lay")
    for out, owner in zip(outs, owners):
        rows = pl.ds(pl.multiple_of(lax.rem(lay + owner, shares) * share, share), share)
        block = lax.dot_general(held[...], store_ref[0, rows, :], NT, preferred_element_type=F32)
        for j in range(out.shape[0] // half):
            out[j * half:(j + 1) * half, :] = block[j * height:j * height + half].astype(out.dtype)


def score(pieces, parts, store, owners):
    half = (pieces + parts)[0].shape[0]
    _, examples, dim = store.shape
    shares = lax.axis_size("lay")
    share = examples // shares
    whole = len(pieces) + (1 if parts else 0)
    height = -(-half // 16) * 16
    vmem = pl.BlockSpec(memory_space=pltpu.VMEM)
    return pl.pallas_call(
        functools.partial(score_kernel, len(pieces), height, share, shares, tuple(owners)),
        out_shape=[jax.ShapeDtypeStruct((whole * half, share), BF16 if owner else F32) for owner in owners],
        in_specs=[vmem] * (len(pieces) + len(parts) + 1),
        out_specs=[vmem] * len(owners),
        scratch_shapes=[pltpu.VMEM((whole * height, dim), BF16)],
        compiler_params=pltpu.CompilerParams(vmem_limit_bytes=24 << 20),
        cost_estimate=pl.CostEstimate(
            flops=2 * 256 * share * len(owners) * dim, bytes_accessed=1 << 20, transcendentals=0
        ),
        name="score",
    )(*pieces, *parts, store)


def swap_layers(sends):
    shares = lax.axis_size("lay")
    return [
        lax.ppermute(send, "lay", [(i, (i + k + 1) % shares) for i in range(shares)])
        for k, send in enumerate(sends)
    ]


def finish_kernel(half, members, sizes, *refs):
    out_ref = refs[-1]
    refs = refs[:-1]
    count = len(sizes)
    each = len(refs) // count
    slab, ex = lax.axis_index("slab"), lax.axis_index("ex")
    place = jnp.where(slab == 0, ex, 2 * members - 1 - ex)
    at = 0
    for k, size in enumerate(sizes):
        keep, got = refs[k * each], refs[k * each + 1:(k + 1) * each]
        for j in range(size):
            rows = slice(j * half, (j + 1) * half)
            total = keep[rows, :]
            for g in got:
                total = total + g[rows, :].astype(F32)
            distance = (at + 1) // 2
            hops = 2 * members - distance if at % 2 == 1 else distance
            source = lax.rem(place + hops, 2 * members)
            block = jnp.where(source < members, 2 * source, 2 * (2 * members - 1 - source) + 1)
            out_ref[pl.ds(pl.multiple_of(block * half, 8), half), :] = total
            at += 1


def finish(half, parts):
    members = lax.axis_size("ex")
    vmem = pl.BlockSpec(memory_space=pltpu.VMEM)
    flat = [array for keep, got in parts for array in [keep, *got]]
    sizes = [keep.shape[0] // half for keep, _ in parts]
    return pl.pallas_call(
        functools.partial(finish_kernel, half, members, sizes),
        out_shape=jax.ShapeDtypeStruct((2 * members * half, flat[0].shape[1]), F32),
        in_specs=[vmem] * len(flat),
        out_specs=vmem,
        compiler_params=pltpu.CompilerParams(vmem_limit_bytes=16 << 20),
        name="finish",
    )(*flat)


def local(
    store_grads, query_grads, query_block, layer_slot, out_basis, in_basis, eigen_values, damping
):
    members = lax.axis_size("ex")
    ring = list(range(members)) + [members + i for i in reversed(range(members))]
    forth = [(a, ring[(i + 1) % len(ring)]) for i, a in enumerate(ring)]
    back = [(b, a) for a, b in forth]
    own, store = rotate(
        query_grads, query_block, layer_slot, out_basis, in_basis, eigen_values, damping, store_grads
    )
    half, dim = own.shape
    others = range(1, lax.axis_size("lay"))
    one = two = own
    batch, sums, hidden = [own], [], []
    for step in range(1, members):
        one, two = lax.ppermute(one, RING, forth), lax.ppermute(two, RING, back)
        if hidden:
            two, hidden = lax.optimization_barrier((two, hidden))
            sums.append((keep, swap_layers(hidden)))
            hidden = []
        batch += [one, two]
        if len(batch) >= 5 and step < members - 1:
            keep, *hidden = score(batch, [], store, [0, *others])
            batch = []
    parts = [lax.ppermute(one[:, :dim // 2], RING, forth), lax.ppermute(two[:, dim // 2:], RING, back)]
    got = swap_layers(score(batch, parts, store, others))
    sums.append((*score(batch, parts, store, [0]), got))
    return finish(half, sums).T


def solution(mesh):
    return jax.shard_map(
        local,
        mesh=mesh,
        in_specs=(
            P("lay", ("slab", "ex"), None),
            P("lay", ("pb", "ex"), None),
            P(),
            P(),
            P(),
            P(),
            P(),
            P(),
        ),
        out_specs=P(("slab", "ex", "lay"), "pb"),
        check_vma=False,
    )
```

```python
import functools

import jax
import jax.numpy as jnp
from jax import lax
from jax.experimental import pallas as pl
from jax.experimental.pallas import tpu as pltpu
from jax.sharding import PartitionSpec as P

RANK = 64
BLOCKS = 4
F32 = jnp.float32
BF16 = jnp.bfloat16
NT = (((1,), (1,)), ((), ()))
RING = ("slab", "ex")


def in_hbm(x):
    return pltpu.with_memory_space_constraint(x, pltpu.HBM)


def split(x):
    hi = x.astype(BF16)
    return hi, (x - hi.astype(F32)).astype(BF16)


def rotate_kernel(
    half, lay_slots, query_hbm, block_hbm, damping_hbm, slot_hbm, out_hbm, in_hbm, eigen_hbm,
    result_ref, query_ref, block_ref, damping_ref, slot_ref, out_ref, in_ref, eigen_ref,
    rows_ref, basis_ref, turned_ref, sems,
):
    pairs = RANK * RANK // 128
    local = query_ref.shape[1]
    copies = [
        pltpu.make_async_copy(source, target, sems.at[k])
        for k, (source, target) in enumerate([
            (slot_hbm, slot_ref), (query_hbm, query_ref), (block_hbm, block_ref), (damping_hbm, damping_ref),
            (out_hbm, out_ref), (in_hbm, in_ref), (eigen_hbm, eigen_ref),
        ])
    ]
    for copy in copies:
        copy.start()
    slab = lax.axis_index("slab")
    first = (lax.axis_index("pb") * lax.axis_size("ex") + lax.axis_index("ex")) * local + slab * half
    low_lanes = lax.broadcasted_iota(jnp.int32, (RANK // 2, 128), 1) < RANK
    row = lax.broadcasted_iota(jnp.int32, (4 * RANK, 4 * RANK), 0) // RANK
    col = lax.broadcasted_iota(jnp.int32, (4 * RANK, 4 * RANK), 1) // RANK
    lane = lax.broadcasted_iota(jnp.int32, (1, 4 * RANK), 1) // RANK
    for copy in copies:
        copy.wait()
    model_layer = slot_ref[lax.axis_index("lay") * lay_slots]

    for pair in range(pairs):
        block = query_ref[0, :, pair * 128:(pair + 1) * 128].astype(F32)
        rows_ref[pair * half:(pair + 1) * half, :] = jnp.where(slab == 0, block[:half], block[half:2 * half])

    basis_ref[:, :RANK] = out_ref[model_layer].astype(F32)
    out_rows = jnp.concatenate(
        [basis_ref[pl.ds(0, RANK // 2, stride=2), :], basis_ref[pl.ds(1, RANK // 2, stride=2), :]], axis=0
    )
    out_t = out_rows.T[:RANK].astype(BF16)
    out_rows = out_rows[:, :RANK].astype(BF16)
    out_twice = jnp.concatenate([out_rows, out_rows], axis=1)
    out_t_twice = jnp.concatenate([out_t, out_t], axis=1)

    in_wide = jnp.concatenate([in_ref[model_layer].astype(F32)] * 4, axis=1)
    in_tall = jnp.concatenate([in_wide] * 4, axis=0)
    in_diag = jnp.where(row == col, in_tall, F32(0.0)).astype(BF16)
    eigen = jnp.concatenate([eigen_ref[model_layer]] * 4, axis=1)

    quads = range(half // 4)
    grids = []
    for quad in quads:
        tops, bottoms = [], []
        for two in range(2):
            at = quad * 4 + two * 2
            a = rows_ref[pl.ds(at, pairs, stride=half), :]
            b = rows_ref[pl.ds(at + 1, pairs, stride=half), :]
            tops.append(jnp.where(low_lanes, a, pltpu.roll(b, RANK, 1)))
            bottoms.append(jnp.where(low_lanes, pltpu.roll(a, RANK, 1), b))
        grids += [jnp.concatenate(tops, axis=1), jnp.concatenate(bottoms, axis=1)]
    right = jnp.dot(jnp.concatenate(grids, axis=0).astype(BF16), in_diag, preferred_element_type=F32)
    turned = []
    for quad in quads:
        part = right[quad * RANK:(quad + 1) * RANK]
        middle = jnp.dot(out_t_twice, jnp.concatenate(split(part), axis=0), preferred_element_type=F32)
        damp = jnp.zeros((1, 4 * RANK), F32)
        for one in range(4):
            block = block_ref[first + quad * 4 + one]
            value = F32(0.0)
            for k in range(BLOCKS):
                value = jnp.where(block == k, damping_ref[k], value)
            damp = jnp.where(lane == one, value, damp)
        scaled = middle / (eigen + damp)
        turned.append(jnp.dot(out_twice, jnp.concatenate(split(scaled), axis=0), preferred_element_type=F32))
    hi, lo = split(jnp.concatenate(turned, axis=0))
    result = lax.dot_general(hi, in_diag, NT, preferred_element_type=F32)
    result = result + lax.dot_general(lo, in_diag, NT, preferred_element_type=F32)
    for quad in quads:
        for two in range(2):
            at = quad * 4 + two * 2
            top = result[quad * RANK:quad * RANK + pairs, two * 128:(two + 1) * 128]
            bottom = result[quad * RANK + pairs:(quad + 1) * RANK, two * 128:(two + 1) * 128]
            turned_ref[pl.ds(at, pairs, stride=half), :] = jnp.where(low_lanes, top, pltpu.roll(bottom, RANK, 1))
            turned_ref[pl.ds(at + 1, pairs, stride=half), :] = jnp.where(low_lanes, pltpu.roll(top, RANK, 1), bottom)

    for pair in range(pairs):
        result_ref[:, pair * 128:(pair + 1) * 128] = turned_ref[pair * half:(pair + 1) * half, :].astype(BF16)


def rotate(query_grads, query_block, layer_slot, out_basis, in_basis, eigen_values, damping):
    half = query_grads.shape[1] // lax.axis_size("slab")
    dim = query_grads.shape[2]
    operands = (query_grads, query_block, damping, layer_slot, out_basis, in_basis, eigen_values)
    homes = (pltpu.VMEM, pltpu.SMEM, pltpu.SMEM, pltpu.SMEM, pltpu.VMEM, pltpu.VMEM, pltpu.VMEM)
    return pl.pallas_call(
        functools.partial(rotate_kernel, half, 1),
        out_shape=jax.ShapeDtypeStruct((half, dim), BF16),
        in_specs=[pl.BlockSpec(memory_space=pltpu.HBM)] * len(operands),
        out_specs=pl.BlockSpec(memory_space=pltpu.VMEM),
        scratch_shapes=[home(x.shape, x.dtype) for home, x in zip(homes, operands)] + [
            pltpu.VMEM((half * dim // 128, 128), F32),
            pltpu.VMEM((RANK, 128), F32),
            pltpu.VMEM((half * dim // 128, 128), F32),
            pltpu.SemaphoreType.DMA((len(operands),)),
        ],
        compiler_params=pltpu.CompilerParams(vmem_limit_bytes=16 << 20),
        cost_estimate=pl.CostEstimate(flops=8 * half * dim * 256, bytes_accessed=1 << 20, transcendentals=0),
        name="rotate",
    )(*map(in_hbm, operands))


def fetch_kernel(after_ref, store_hbm, store_ref, sems):
    del after_ref
    parts = sems.shape[0]
    rows = store_ref.shape[1] // parts
    copies = [
        pltpu.make_async_copy(
            store_hbm.at[:, pl.ds(k * rows, rows)], store_ref.at[:, pl.ds(k * rows, rows)], sems.at[k]
        )
        for k in range(parts)
    ]
    for copy in copies:
        copy.start()
    for copy in copies:
        copy.wait()


def fetch(after, store):
    return pl.pallas_call(
        fetch_kernel,
        out_shape=jax.ShapeDtypeStruct(store.shape, store.dtype),
        in_specs=[pl.BlockSpec(memory_space=pltpu.VMEM), pl.BlockSpec(memory_space=pltpu.HBM)],
        out_specs=pl.BlockSpec(memory_space=pltpu.VMEM),
        scratch_shapes=[pltpu.SemaphoreType.DMA((4,))],
        compiler_params=pltpu.CompilerParams(vmem_limit_bytes=8 << 20),
        cost_estimate=pl.CostEstimate(flops=0, bytes_accessed=2 * store.size * 2, transcendentals=0),
        name="fetch",
    )(after, in_hbm(store))


def score_kernel(count, height, share, shares, owners, *refs):
    pieces, store_ref, held = refs[:count], refs[count], refs[-1]
    before, outs = refs[count + 1:-1 - len(owners)], refs[-1 - len(owners):-1]
    half = pieces[0].shape[0]
    for k, piece in enumerate(pieces):
        held[k * height:k * height + half, :] = piece[...]
    lay = lax.axis_index("lay")
    for i, (out, owner) in enumerate(zip(outs, owners)):
        rows = pl.ds(pl.multiple_of(lax.rem(lay + owner, shares) * share, share), share)
        block = lax.dot_general(held[...], store_ref[0, rows, :], NT, preferred_element_type=F32)
        start = out.shape[0] - count * half
        if start:
            out[:start, :] = before[i][...]
        for j in range(count):
            out[start + j * half:start + (j + 1) * half, :] = block[j * height:j * height + half].astype(out.dtype)


def score(pieces, store, owners, before=()):
    half, dim = pieces[0].shape
    shares = lax.axis_size("lay")
    share = store.shape[1] // shares
    count = len(pieces)
    height = -(-half // 16) * 16
    rows = count * half + (before[0].shape[0] if before else 0)
    vmem = pl.BlockSpec(memory_space=pltpu.VMEM)
    return pl.pallas_call(
        functools.partial(score_kernel, count, height, share, shares, tuple(owners)),
        out_shape=[jax.ShapeDtypeStruct((rows, share), BF16 if owner else F32) for owner in owners],
        in_specs=[vmem] * (count + 1 + len(before)),
        out_specs=[vmem] * len(owners),
        scratch_shapes=[pltpu.VMEM((count * height, dim), BF16)],
        compiler_params=pltpu.CompilerParams(vmem_limit_bytes=24 << 20),
        cost_estimate=pl.CostEstimate(
            flops=2 * 256 * share * len(owners) * dim, bytes_accessed=1 << 20, transcendentals=0
        ),
        name="score",
    )(*pieces, store, *before)


def swap_layers(sends):
    shares = lax.axis_size("lay")
    return [
        lax.ppermute(send, "lay", [(i, (i + k + 1) % shares) for i in range(shares)])
        for k, send in enumerate(sends)
    ]


def finish_kernel(half, members, sizes, *refs):
    out_ref = refs[-1]
    refs = refs[:-1]
    count = len(sizes)
    each = len(refs) // count
    slab, ex = lax.axis_index("slab"), lax.axis_index("ex")
    place = jnp.where(slab == 0, ex, 2 * members - 1 - ex)
    at = 0
    for k, size in enumerate(sizes):
        keep, got = refs[k * each], refs[k * each + 1:(k + 1) * each]
        for j in range(size):
            rows = slice(j * half, (j + 1) * half)
            total = keep[rows, :]
            for g in got:
                total = total + g[rows, :].astype(F32)
            distance = (at + 1) // 2
            hops = 2 * members - distance if at % 2 == 1 else distance
            source = lax.rem(place + hops, 2 * members)
            block = jnp.where(source < members, 2 * source, 2 * (2 * members - 1 - source) + 1)
            out_ref[pl.ds(pl.multiple_of(block * half, 8), half), :] = total
            at += 1


def finish(half, parts):
    members = lax.axis_size("ex")
    vmem = pl.BlockSpec(memory_space=pltpu.VMEM)
    flat = [array for keep, got in parts for array in [keep, *got]]
    sizes = [keep.shape[0] // half for keep, _ in parts]
    return pl.pallas_call(
        functools.partial(finish_kernel, half, members, sizes),
        out_shape=jax.ShapeDtypeStruct((2 * members * half, flat[0].shape[1]), F32),
        in_specs=[vmem] * len(flat),
        out_specs=vmem,
        compiler_params=pltpu.CompilerParams(vmem_limit_bytes=16 << 20),
        name="finish",
    )(*flat)


def local(
    store_grads, query_grads, query_block, layer_slot, out_basis, in_basis, eigen_values, damping
):
    members = lax.axis_size("ex")
    ring = list(range(members)) + [members + i for i in reversed(range(members))]
    forth = [(a, ring[(i + 1) % len(ring)]) for i, a in enumerate(ring)]
    back = [(b, a) for a, b in forth]
    own = rotate(query_grads, query_block, layer_slot, out_basis, in_basis, eigen_values, damping)
    store = fetch(own, store_grads)
    half, _ = own.shape
    others = range(1, lax.axis_size("lay"))
    one = two = own
    batch, sums, hidden = [own], [], [store]
    for step in range(1, members):
        one, two = lax.ppermute(one, RING, forth), lax.ppermute(two, RING, back)
        one, hidden = lax.optimization_barrier((one, hidden))
        if step == 1:
            store, = hidden
            hidden = []
        batch += [one, two]
        if len(batch) >= 5 or step == members - 1:
            if hidden and step < members - 1:
                keep, *sends = hidden
                sums.append((keep, swap_layers(sends)))
                hidden = []
            hidden = score(batch, store, [0, *others], hidden)
            batch = []
    keep, *sends = hidden
    sums.append((keep, swap_layers(sends)))
    last = [lax.ppermute(one, RING, forth)]
    got = swap_layers(score(last, store, others))
    sums.append((*score(last, store, [0]), got))
    return finish(half, sums).T


def solution(mesh):
    return jax.shard_map(
        local,
        mesh=mesh,
        in_specs=(
            P("lay", ("slab", "ex"), None),
            P("lay", ("pb", "ex"), None),
            P(),
            P(),
            P(),
            P(),
            P(),
            P(),
        ),
        out_specs=P(("slab", "ex", "lay"), "pb"),
        check_vma=False,
    )
```

```python
import functools

import jax
import jax.numpy as jnp
from jax import lax
from jax.experimental import pallas as pl
from jax.experimental.pallas import tpu as pltpu
from jax.sharding import PartitionSpec as P

RANK = 64
BLOCKS = 4
F32 = jnp.float32
BF16 = jnp.bfloat16
NT = (((1,), (1,)), ((), ()))
RING = ("slab", "ex")


def in_hbm(x):
    return pltpu.with_memory_space_constraint(x, pltpu.HBM)


def split(x):
    hi = x.astype(BF16)
    return hi, (x - hi.astype(F32)).astype(BF16)


def rotate_kernel(
    half, lay_slots, query_hbm, block_hbm, damping_hbm, slot_hbm, out_hbm, in_hbm, eigen_hbm,
    result_ref, query_ref, block_ref, damping_ref, slot_ref, out_ref, in_ref, eigen_ref,
    rows_ref, basis_ref, turned_ref, sems,
):
    pairs = RANK * RANK // 128
    local = query_ref.shape[1]
    copies = [
        pltpu.make_async_copy(source, target, sems.at[k])
        for k, (source, target) in enumerate([
            (slot_hbm, slot_ref), (query_hbm, query_ref), (block_hbm, block_ref), (damping_hbm, damping_ref),
            (out_hbm, out_ref), (in_hbm, in_ref), (eigen_hbm, eigen_ref),
        ])
    ]
    for copy in copies:
        copy.start()
    slab = lax.axis_index("slab")
    first = (lax.axis_index("pb") * lax.axis_size("ex") + lax.axis_index("ex")) * local + slab * half
    low_lanes = lax.broadcasted_iota(jnp.int32, (RANK // 2, 128), 1) < RANK
    row = lax.broadcasted_iota(jnp.int32, (4 * RANK, 4 * RANK), 0) // RANK
    col = lax.broadcasted_iota(jnp.int32, (4 * RANK, 4 * RANK), 1) // RANK
    lane = lax.broadcasted_iota(jnp.int32, (1, 4 * RANK), 1) // RANK
    for copy in copies:
        copy.wait()
    model_layer = slot_ref[lax.axis_index("lay") * lay_slots]

    for pair in range(pairs):
        block = query_ref[0, :, pair * 128:(pair + 1) * 128].astype(F32)
        rows_ref[pair * half:(pair + 1) * half, :] = jnp.where(slab == 0, block[:half], block[half:2 * half])

    basis_ref[:, :RANK] = out_ref[model_layer].astype(F32)
    out_rows = jnp.concatenate(
        [basis_ref[pl.ds(0, RANK // 2, stride=2), :], basis_ref[pl.ds(1, RANK // 2, stride=2), :]], axis=0
    )
    out_t = out_rows.T[:RANK].astype(BF16)
    out_rows = out_rows[:, :RANK].astype(BF16)
    out_twice = jnp.concatenate([out_rows, out_rows], axis=1)
    out_t_twice = jnp.concatenate([out_t, out_t], axis=1)

    in_wide = jnp.concatenate([in_ref[model_layer].astype(F32)] * 4, axis=1)
    in_tall = jnp.concatenate([in_wide] * 4, axis=0)
    in_diag = jnp.where(row == col, in_tall, F32(0.0)).astype(BF16)
    eigen = jnp.concatenate([eigen_ref[model_layer]] * 4, axis=1)

    quads = range(half // 4)
    grids = []
    for quad in quads:
        tops, bottoms = [], []
        for two in range(2):
            at = quad * 4 + two * 2
            a = rows_ref[pl.ds(at, pairs, stride=half), :]
            b = rows_ref[pl.ds(at + 1, pairs, stride=half), :]
            tops.append(jnp.where(low_lanes, a, pltpu.roll(b, RANK, 1)))
            bottoms.append(jnp.where(low_lanes, pltpu.roll(a, RANK, 1), b))
        grids += [jnp.concatenate(tops, axis=1), jnp.concatenate(bottoms, axis=1)]
    right = jnp.dot(jnp.concatenate(grids, axis=0).astype(BF16), in_diag, preferred_element_type=F32)
    middles = [
        jnp.dot(
            out_t_twice, jnp.concatenate(split(right[quad * RANK:(quad + 1) * RANK]), axis=0),
            preferred_element_type=F32,
        )
        for quad in quads
    ]
    scaled = []
    for quad in quads:
        damp = jnp.zeros((1, 4 * RANK), F32)
        for one in range(4):
            block = block_ref[first + quad * 4 + one]
            value = F32(0.0)
            for k in range(BLOCKS):
                value = jnp.where(block == k, damping_ref[k], value)
            damp = jnp.where(lane == one, value, damp)
        scaled.append(middles[quad] / (eigen + damp))
    turned = [
        jnp.dot(out_twice, jnp.concatenate(split(block), axis=0), preferred_element_type=F32) for block in scaled
    ]
    hi, lo = split(jnp.concatenate(turned, axis=0))
    result = lax.dot_general(hi, in_diag, NT, preferred_element_type=F32)
    result = result + lax.dot_general(lo, in_diag, NT, preferred_element_type=F32)
    for quad in quads:
        for two in range(2):
            at = quad * 4 + two * 2
            top = result[quad * RANK:quad * RANK + pairs, two * 128:(two + 1) * 128]
            bottom = result[quad * RANK + pairs:(quad + 1) * RANK, two * 128:(two + 1) * 128]
            turned_ref[pl.ds(at, pairs, stride=half), :] = jnp.where(low_lanes, top, pltpu.roll(bottom, RANK, 1))
            turned_ref[pl.ds(at + 1, pairs, stride=half), :] = jnp.where(low_lanes, pltpu.roll(top, RANK, 1), bottom)

    for pair in range(pairs):
        result_ref[:, pair * 128:(pair + 1) * 128] = turned_ref[pair * half:(pair + 1) * half, :].astype(BF16)


def rotate(query_grads, query_block, layer_slot, out_basis, in_basis, eigen_values, damping):
    half = query_grads.shape[1] // lax.axis_size("slab")
    dim = query_grads.shape[2]
    operands = (query_grads, query_block, damping, layer_slot, out_basis, in_basis, eigen_values)
    homes = (pltpu.VMEM, pltpu.SMEM, pltpu.SMEM, pltpu.SMEM, pltpu.VMEM, pltpu.VMEM, pltpu.VMEM)
    return pl.pallas_call(
        functools.partial(rotate_kernel, half, 1),
        out_shape=jax.ShapeDtypeStruct((half, dim), BF16),
        in_specs=[pl.BlockSpec(memory_space=pltpu.HBM)] * len(operands),
        out_specs=pl.BlockSpec(memory_space=pltpu.VMEM),
        scratch_shapes=[home(x.shape, x.dtype) for home, x in zip(homes, operands)] + [
            pltpu.VMEM((half * dim // 128, 128), F32),
            pltpu.VMEM((RANK, 128), F32),
            pltpu.VMEM((half * dim // 128, 128), F32),
            pltpu.SemaphoreType.DMA((len(operands),)),
        ],
        compiler_params=pltpu.CompilerParams(vmem_limit_bytes=16 << 20),
        cost_estimate=pl.CostEstimate(flops=8 * half * dim * 256, bytes_accessed=1 << 20, transcendentals=0),
        name="rotate",
    )(*map(in_hbm, operands))


def fetch_kernel(after_ref, store_hbm, store_ref, sems):
    del after_ref
    parts = sems.shape[0]
    rows = store_ref.shape[1] // parts
    copies = [
        pltpu.make_async_copy(
            store_hbm.at[:, pl.ds(k * rows, rows)], store_ref.at[:, pl.ds(k * rows, rows)], sems.at[k]
        )
        for k in range(parts)
    ]
    for copy in copies:
        copy.start()
    for copy in copies:
        copy.wait()


def fetch(after, store):
    return pl.pallas_call(
        fetch_kernel,
        out_shape=jax.ShapeDtypeStruct(store.shape, store.dtype),
        in_specs=[pl.BlockSpec(memory_space=pltpu.VMEM), pl.BlockSpec(memory_space=pltpu.HBM)],
        out_specs=pl.BlockSpec(memory_space=pltpu.VMEM),
        scratch_shapes=[pltpu.SemaphoreType.DMA((4,))],
        compiler_params=pltpu.CompilerParams(vmem_limit_bytes=8 << 20),
        cost_estimate=pl.CostEstimate(flops=0, bytes_accessed=2 * store.size * 2, transcendentals=0),
        name="fetch",
    )(after, in_hbm(store))


def score_kernel(count, height, share, shares, owners, *refs):
    outs, held = refs[-1 - len(owners):-1], refs[-1]
    pieces, store_ref = refs[:-2 - len(owners)], refs[-2 - len(owners)]
    half = pieces[0].shape[0]
    for k, piece in enumerate(pieces[:count]):
        held[k * height:k * height + half, :] = piece[...]
    column = 0
    for piece in pieces[count:]:
        held[count * height:count * height + half, column:column + piece.shape[1]] = piece[...]
        column += piece.shape[1]
    lay = lax.axis_index("lay")
    for out, owner in zip(outs, owners):
        rows = pl.ds(pl.multiple_of(lax.rem(lay + owner, shares) * share, share), share)
        block = lax.dot_general(held[...], store_ref[0, rows, :], NT, preferred_element_type=F32)
        for j in range(out.shape[0] // half):
            out[j * half:(j + 1) * half, :] = block[j * height:j * height + half].astype(out.dtype)


def score(pieces, parts, store, owners):
    half = (pieces + parts)[0].shape[0]
    _, examples, dim = store.shape
    shares = lax.axis_size("lay")
    share = examples // shares
    whole = len(pieces) + (1 if parts else 0)
    height = -(-half // 16) * 16
    vmem = pl.BlockSpec(memory_space=pltpu.VMEM)
    return pl.pallas_call(
        functools.partial(score_kernel, len(pieces), height, share, shares, tuple(owners)),
        out_shape=[jax.ShapeDtypeStruct((whole * half, share), BF16 if owner else F32) for owner in owners],
        in_specs=[vmem] * (len(pieces) + len(parts) + 1),
        out_specs=[vmem] * len(owners),
        scratch_shapes=[pltpu.VMEM((whole * height, dim), BF16)],
        compiler_params=pltpu.CompilerParams(vmem_limit_bytes=24 << 20),
        cost_estimate=pl.CostEstimate(
            flops=2 * 256 * share * len(owners) * dim, bytes_accessed=1 << 20, transcendentals=0
        ),
        name="score",
    )(*pieces, *parts, store)


def swap_layers(sends):
    shares = lax.axis_size("lay")
    return [
        lax.ppermute(send, "lay", [(i, (i + k + 1) % shares) for i in range(shares)])
        for k, send in enumerate(sends)
    ]


def finish_kernel(half, members, sizes, *refs):
    out_ref = refs[-1]
    refs = refs[:-1]
    count = len(sizes)
    each = len(refs) // count
    slab, ex = lax.axis_index("slab"), lax.axis_index("ex")
    place = jnp.where(slab == 0, ex, 2 * members - 1 - ex)
    at = 0
    for k, size in enumerate(sizes):
        keep, got = refs[k * each], refs[k * each + 1:(k + 1) * each]
        for j in range(size):
            rows = slice(j * half, (j + 1) * half)
            total = keep[rows, :]
            for g in got:
                total = total + g[rows, :].astype(F32)
            distance = (at + 1) // 2
            hops = 2 * members - distance if at % 2 == 1 else distance
            source = lax.rem(place + hops, 2 * members)
            block = jnp.where(source < members, 2 * source, 2 * (2 * members - 1 - source) + 1)
            out_ref[pl.ds(pl.multiple_of(block * half, 8), half), :] = total
            at += 1


def finish(half, parts):
    members = lax.axis_size("ex")
    vmem = pl.BlockSpec(memory_space=pltpu.VMEM)
    flat = [array for keep, got in parts for array in [keep, *got]]
    sizes = [keep.shape[0] // half for keep, _ in parts]
    return pl.pallas_call(
        functools.partial(finish_kernel, half, members, sizes),
        out_shape=jax.ShapeDtypeStruct((2 * members * half, flat[0].shape[1]), F32),
        in_specs=[vmem] * len(flat),
        out_specs=vmem,
        compiler_params=pltpu.CompilerParams(vmem_limit_bytes=16 << 20),
        name="finish",
    )(*flat)


def local(
    store_grads, query_grads, query_block, layer_slot, out_basis, in_basis, eigen_values, damping
):
    members = lax.axis_size("ex")
    ring = list(range(members)) + [members + i for i in reversed(range(members))]
    def hop(piece, steps):
        return lax.ppermute(piece, RING, [(a, ring[(i + steps) % len(ring)]) for i, a in enumerate(ring)])

    own = rotate(query_grads, query_block, layer_slot, out_basis, in_basis, eigen_values, damping)
    store = fetch(own, store_grads)
    half, dim = own.shape
    others = range(1, lax.axis_size("lay"))
    one = two = own
    batch, sums, hidden = [own], [], [store]
    for step in range(1, members):
        if step == members - 1:
            cut = dim // 8 * 5 // 128 * 128
            parts = [one[:, :cut], two[:, cut:]]
        one, two = hop(one, 1), hop(two, -1)
        if step == members - 1:
            parts = [hop(parts[0], 2), hop(parts[1], -2)]
        if step < members - 1:
            one, hidden = lax.optimization_barrier((one, hidden))
        if step == 1:
            store, = hidden
        elif hidden:
            keep, *sends = hidden
            sums.append((keep, swap_layers(sends)))
        hidden = []
        batch += [one, two]
        if len(batch) >= 5 and step < members - 1:
            hidden = score(batch, [], store, [0, *others])
            batch = []
    got = swap_layers(score(batch, parts, store, others))
    sums.append((*score(batch, parts, store, [0]), got))
    return finish(half, sums).T


def solution(mesh):
    return jax.shard_map(
        local,
        mesh=mesh,
        in_specs=(
            P("lay", ("slab", "ex"), None),
            P("lay", ("pb", "ex"), None),
            P(),
            P(),
            P(),
            P(),
            P(),
            P(),
        ),
        out_specs=P(("slab", "ex", "lay"), "pb"),
        check_vma=False,
    )
```

```python
import functools

import jax
import jax.numpy as jnp
from jax import lax
from jax.experimental import pallas as pl
from jax.experimental.pallas import tpu as pltpu
from jax.sharding import PartitionSpec as P

RANK = 64
BLOCKS = 4
F32 = jnp.float32
BF16 = jnp.bfloat16
NT = (((1,), (1,)), ((), ()))
RING = ("slab", "ex")


def in_hbm(x):
    return pltpu.with_memory_space_constraint(x, pltpu.HBM)


def split(x):
    hi = x.astype(BF16)
    return hi, (x - hi.astype(F32)).astype(BF16)


def rotate_kernel(
    half, lay_slots, query_hbm, block_hbm, damping_hbm, slot_hbm, out_hbm, in_hbm, eigen_hbm,
    result_ref, query_ref, block_ref, damping_ref, slot_ref, out_ref, in_ref, eigen_ref,
    rows_ref, basis_ref, turned_ref, sems,
):
    pairs = RANK * RANK // 128
    local = query_ref.shape[1]
    copies = [
        pltpu.make_async_copy(source, target, sems.at[k])
        for k, (source, target) in enumerate([
            (slot_hbm, slot_ref), (query_hbm, query_ref), (block_hbm, block_ref), (damping_hbm, damping_ref),
            (out_hbm, out_ref), (in_hbm, in_ref), (eigen_hbm, eigen_ref),
        ])
    ]
    for copy in copies:
        copy.start()
    slab = lax.axis_index("slab")
    first = (lax.axis_index("pb") * lax.axis_size("ex") + lax.axis_index("ex")) * local + slab * half
    low_lanes = lax.broadcasted_iota(jnp.int32, (RANK // 2, 128), 1) < RANK
    row = lax.broadcasted_iota(jnp.int32, (4 * RANK, 4 * RANK), 0) // RANK
    col = lax.broadcasted_iota(jnp.int32, (4 * RANK, 4 * RANK), 1) // RANK
    lane = lax.broadcasted_iota(jnp.int32, (1, 4 * RANK), 1) // RANK
    for copy in copies:
        copy.wait()
    model_layer = slot_ref[lax.axis_index("lay") * lay_slots]

    for pair in range(pairs):
        block = query_ref[0, :, pair * 128:(pair + 1) * 128].astype(F32)
        rows_ref[pair * half:(pair + 1) * half, :] = jnp.where(slab == 0, block[:half], block[half:2 * half])

    basis_ref[:, :RANK] = out_ref[model_layer].astype(F32)
    out_rows = jnp.concatenate(
        [basis_ref[pl.ds(0, RANK // 2, stride=2), :], basis_ref[pl.ds(1, RANK // 2, stride=2), :]], axis=0
    )
    out_t = out_rows.T[:RANK].astype(BF16)
    out_rows = out_rows[:, :RANK].astype(BF16)
    out_twice = jnp.concatenate([out_rows, out_rows], axis=1)
    out_t_twice = jnp.concatenate([out_t, out_t], axis=1)

    in_wide = jnp.concatenate([in_ref[model_layer].astype(F32)] * 4, axis=1)
    in_tall = jnp.concatenate([in_wide] * 4, axis=0)
    in_diag = jnp.where(row == col, in_tall, F32(0.0)).astype(BF16)
    eigen = jnp.concatenate([eigen_ref[model_layer]] * 4, axis=1)

    quads = range(half // 4)
    grids = []
    for quad in quads:
        tops, bottoms = [], []
        for two in range(2):
            at = quad * 4 + two * 2
            a = rows_ref[pl.ds(at, pairs, stride=half), :]
            b = rows_ref[pl.ds(at + 1, pairs, stride=half), :]
            tops.append(jnp.where(low_lanes, a, pltpu.roll(b, RANK, 1)))
            bottoms.append(jnp.where(low_lanes, pltpu.roll(a, RANK, 1), b))
        grids += [jnp.concatenate(tops, axis=1), jnp.concatenate(bottoms, axis=1)]
    right = jnp.dot(jnp.concatenate(grids, axis=0).astype(BF16), in_diag, preferred_element_type=F32)
    middles = [
        jnp.dot(
            out_t_twice, jnp.concatenate(split(right[quad * RANK:(quad + 1) * RANK]), axis=0),
            preferred_element_type=F32,
        )
        for quad in quads
    ]
    scaled = []
    for quad in quads:
        damp = jnp.zeros((1, 4 * RANK), F32)
        for one in range(4):
            block = block_ref[first + quad * 4 + one]
            value = F32(0.0)
            for k in range(BLOCKS):
                value = jnp.where(block == k, damping_ref[k], value)
            damp = jnp.where(lane == one, value, damp)
        scaled.append(middles[quad] / (eigen + damp))
    turned = [
        jnp.dot(out_twice, jnp.concatenate(split(block), axis=0), preferred_element_type=F32) for block in scaled
    ]
    hi, lo = split(jnp.concatenate(turned, axis=0))
    result = lax.dot_general(hi, in_diag, NT, preferred_element_type=F32)
    result = result + lax.dot_general(lo, in_diag, NT, preferred_element_type=F32)
    for quad in quads:
        for two in range(2):
            at = quad * 4 + two * 2
            top = result[quad * RANK:quad * RANK + pairs, two * 128:(two + 1) * 128]
            bottom = result[quad * RANK + pairs:(quad + 1) * RANK, two * 128:(two + 1) * 128]
            turned_ref[pl.ds(at, pairs, stride=half), :] = jnp.where(low_lanes, top, pltpu.roll(bottom, RANK, 1))
            turned_ref[pl.ds(at + 1, pairs, stride=half), :] = jnp.where(low_lanes, pltpu.roll(top, RANK, 1), bottom)

    for pair in range(pairs):
        result_ref[:, pair * 128:(pair + 1) * 128] = turned_ref[pair * half:(pair + 1) * half, :].astype(BF16)


def rotate(query_grads, query_block, layer_slot, out_basis, in_basis, eigen_values, damping):
    half = query_grads.shape[1] // lax.axis_size("slab")
    dim = query_grads.shape[2]
    operands = (query_grads, query_block, damping, layer_slot, out_basis, in_basis, eigen_values)
    homes = (pltpu.VMEM, pltpu.SMEM, pltpu.SMEM, pltpu.SMEM, pltpu.VMEM, pltpu.VMEM, pltpu.VMEM)
    return pl.pallas_call(
        functools.partial(rotate_kernel, half, 1),
        out_shape=jax.ShapeDtypeStruct((half, dim), BF16),
        in_specs=[pl.BlockSpec(memory_space=pltpu.HBM)] * len(operands),
        out_specs=pl.BlockSpec(memory_space=pltpu.VMEM),
        scratch_shapes=[home(x.shape, x.dtype) for home, x in zip(homes, operands)] + [
            pltpu.VMEM((half * dim // 128, 128), F32),
            pltpu.VMEM((RANK, 128), F32),
            pltpu.VMEM((half * dim // 128, 128), F32),
            pltpu.SemaphoreType.DMA((len(operands),)),
        ],
        compiler_params=pltpu.CompilerParams(vmem_limit_bytes=16 << 20),
        cost_estimate=pl.CostEstimate(flops=8 * half * dim * 256, bytes_accessed=1 << 20, transcendentals=0),
        name="rotate",
    )(*map(in_hbm, operands))


def fetch_kernel(shares, after_ref, store_hbm, store_ref, turned_ref, sems):
    del after_ref
    parts = sems.shape[0]
    rows = store_ref.shape[1] // parts
    copies = [
        pltpu.make_async_copy(
            store_hbm.at[:, pl.ds(k * rows, rows)], store_ref.at[:, pl.ds(k * rows, rows)], sems.at[k]
        )
        for k in range(parts)
    ]
    for copy in copies:
        copy.start()
    for copy in copies:
        copy.wait()
    lay = lax.axis_index("lay")
    for k in range(shares - 1):
        share = turned_ref.shape[2]
        owned = pl.ds(pl.multiple_of(lax.rem(lay + k + 1, shares) * share, share), share)
        turned_ref[k] = store_ref[0, owned, :].T


def fetch(after, store):
    shares = lax.axis_size("lay")
    _, examples, dim = store.shape
    vmem = pl.BlockSpec(memory_space=pltpu.VMEM)
    return pl.pallas_call(
        functools.partial(fetch_kernel, shares),
        out_shape=[
            jax.ShapeDtypeStruct(store.shape, store.dtype),
            jax.ShapeDtypeStruct((shares - 1, dim, examples // shares), store.dtype),
        ],
        in_specs=[vmem, pl.BlockSpec(memory_space=pltpu.HBM)],
        out_specs=[vmem] * 2,
        scratch_shapes=[pltpu.SemaphoreType.DMA((4,))],
        compiler_params=pltpu.CompilerParams(vmem_limit_bytes=24 << 20),
        cost_estimate=pl.CostEstimate(flops=0, bytes_accessed=2 * store.size * 2, transcendentals=0),
        name="fetch",
    )(after, in_hbm(store))


def score_kernel(count, height, share, shares, owners, turned, *refs):
    outs, held = refs[-1 - len(owners):-1], refs[-1]
    pieces, store_ref = refs[:-2 - len(owners)], refs[-2 - len(owners)]
    half = pieces[0].shape[0]
    for k, piece in enumerate(pieces[:count]):
        held[k * height:k * height + half, :] = piece[...]
    column = 0
    for piece in pieces[count:]:
        held[count * height:count * height + half, column:column + piece.shape[1]] = piece[...]
        column += piece.shape[1]
    lay = lax.axis_index("lay")
    for out, owner in zip(outs, owners):
        if not turned:
            rows = pl.ds(pl.multiple_of(lax.rem(lay + owner, shares) * share, share), share)
            block = lax.dot_general(held[...], store_ref[0, rows, :], NT, preferred_element_type=F32)
        else:
            block = jnp.dot(held[...], store_ref[owner - 1], preferred_element_type=F32)
        for j in range(out.shape[0] // half):
            out[j * half:(j + 1) * half, :] = block[j * height:j * height + half].astype(out.dtype)


def score(pieces, parts, store, owners, turned=False):
    half, dim = pieces[0].shape
    shares = lax.axis_size("lay")
    share = store.shape[2] if turned else store.shape[1] // shares
    whole = len(pieces) + (1 if parts else 0)
    height = -(-half // 16) * 16
    vmem = pl.BlockSpec(memory_space=pltpu.VMEM)
    return pl.pallas_call(
        functools.partial(score_kernel, len(pieces), height, share, shares, tuple(owners), turned),
        out_shape=[jax.ShapeDtypeStruct((whole * half, share), BF16 if owner else F32) for owner in owners],
        in_specs=[vmem] * (len(pieces) + len(parts) + 1),
        out_specs=[vmem] * len(owners),
        scratch_shapes=[pltpu.VMEM((whole * height, dim), BF16)],
        compiler_params=pltpu.CompilerParams(vmem_limit_bytes=24 << 20),
        cost_estimate=pl.CostEstimate(
            flops=2 * 256 * share * len(owners) * dim, bytes_accessed=1 << 20, transcendentals=0
        ),
        name="score",
    )(*pieces, *parts, store)


def swap_layers(sends):
    shares = lax.axis_size("lay")
    return [
        lax.ppermute(send, "lay", [(i, (i + k + 1) % shares) for i in range(shares)])
        for k, send in enumerate(sends)
    ]


def finish_kernel(half, members, sizes, *refs):
    out_ref = refs[-1]
    refs = refs[:-1]
    count = len(sizes)
    each = len(refs) // count
    slab, ex = lax.axis_index("slab"), lax.axis_index("ex")
    place = jnp.where(slab == 0, ex, 2 * members - 1 - ex)
    at = 0
    for k, size in enumerate(sizes):
        keep, got = refs[k * each], refs[k * each + 1:(k + 1) * each]
        for j in range(size):
            rows = slice(j * half, (j + 1) * half)
            total = keep[rows, :]
            for g in got:
                total = total + g[rows, :].astype(F32)
            distance = (at + 1) // 2
            hops = 2 * members - distance if at % 2 == 1 else distance
            source = lax.rem(place + hops, 2 * members)
            block = jnp.where(source < members, 2 * source, 2 * (2 * members - 1 - source) + 1)
            out_ref[pl.ds(pl.multiple_of(block * half, 8), half), :] = total
            at += 1


def finish(half, parts):
    members = lax.axis_size("ex")
    vmem = pl.BlockSpec(memory_space=pltpu.VMEM)
    flat = [array for keep, got in parts for array in [keep, *got]]
    sizes = [keep.shape[0] // half for keep, _ in parts]
    return pl.pallas_call(
        functools.partial(finish_kernel, half, members, sizes),
        out_shape=jax.ShapeDtypeStruct((2 * members * half, flat[0].shape[1]), F32),
        in_specs=[vmem] * len(flat),
        out_specs=vmem,
        compiler_params=pltpu.CompilerParams(vmem_limit_bytes=16 << 20),
        name="finish",
    )(*flat)


def local(
    store_grads, query_grads, query_block, layer_slot, out_basis, in_basis, eigen_values, damping
):
    members = lax.axis_size("ex")
    ring = list(range(members)) + [members + i for i in reversed(range(members))]
    def hop(piece, steps):
        return lax.ppermute(piece, RING, [(a, ring[(i + steps) % len(ring)]) for i, a in enumerate(ring)])

    own = rotate(query_grads, query_block, layer_slot, out_basis, in_basis, eigen_values, damping)
    store, turned = fetch(own, store_grads)
    half, dim = own.shape
    others = range(1, lax.axis_size("lay"))
    one = two = own
    batch, sums, hidden = [own], [], [store, turned]
    for step in range(1, members):
        if step == members - 1:
            cut = dim // 8 * 5 // 128 * 128
            parts = [one[:, :cut], two[:, cut:]]
        one, two = hop(one, 1), hop(two, -1)
        if step == members - 1:
            parts = [hop(parts[0], 2), hop(parts[1], -2)]
        if step < members - 1:
            one, hidden = lax.optimization_barrier((one, hidden))
        if step == 1:
            store, turned = hidden
        elif hidden:
            keep, *sends = hidden
            sums.append((keep, swap_layers(sends)))
        hidden = []
        batch += [one, two]
        if len(batch) >= 5 and step < members - 1:
            hidden = score(batch, [], store, [0, *others])
            batch = []
    got = swap_layers(score(batch, parts, turned, others, True))
    sums.append((*score(batch, parts, store, [0]), got))
    return finish(half, sums).T


def solution(mesh):
    return jax.shard_map(
        local,
        mesh=mesh,
        in_specs=(
            P("lay", ("slab", "ex"), None),
            P("lay", ("pb", "ex"), None),
            P(),
            P(),
            P(),
            P(),
            P(),
            P(),
        ),
        out_specs=P(("slab", "ex", "lay"), "pb"),
        check_vma=False,
    )
```

```python
import functools

import jax
import jax.numpy as jnp
from jax import lax
from jax.experimental import pallas as pl
from jax.experimental.pallas import tpu as pltpu
from jax.sharding import PartitionSpec as P

RANK = 64
BLOCKS = 4
F32 = jnp.float32
BF16 = jnp.bfloat16
NT = (((1,), (1,)), ((), ()))
RING = ("slab", "ex")


def in_hbm(x):
    return pltpu.with_memory_space_constraint(x, pltpu.HBM)


def split(x):
    hi = x.astype(BF16)
    return hi, (x - hi.astype(F32)).astype(BF16)


def rotate_kernel(
    half, lay_slots, query_hbm, block_hbm, damping_hbm, slot_hbm, out_hbm, in_hbm, eigen_hbm,
    result_ref, query_ref, block_ref, damping_ref, slot_ref, out_ref, in_ref, eigen_ref,
    rows_ref, basis_ref, turned_ref, sems,
):
    pairs = RANK * RANK // 128
    local = query_ref.shape[1]
    copies = [
        pltpu.make_async_copy(source, target, sems.at[k])
        for k, (source, target) in enumerate([
            (slot_hbm, slot_ref), (query_hbm, query_ref), (block_hbm, block_ref), (damping_hbm, damping_ref),
            (out_hbm, out_ref), (in_hbm, in_ref), (eigen_hbm, eigen_ref),
        ])
    ]
    for copy in copies:
        copy.start()
    slab = lax.axis_index("slab")
    first = (lax.axis_index("pb") * lax.axis_size("ex") + lax.axis_index("ex")) * local + slab * half
    low_lanes = lax.broadcasted_iota(jnp.int32, (RANK // 2, 128), 1) < RANK
    row = lax.broadcasted_iota(jnp.int32, (4 * RANK, 4 * RANK), 0) // RANK
    col = lax.broadcasted_iota(jnp.int32, (4 * RANK, 4 * RANK), 1) // RANK
    lane = lax.broadcasted_iota(jnp.int32, (1, 4 * RANK), 1) // RANK
    for copy in copies:
        copy.wait()
    model_layer = slot_ref[lax.axis_index("lay") * lay_slots]

    for pair in range(pairs):
        block = query_ref[0, :, pair * 128:(pair + 1) * 128].astype(F32)
        rows_ref[pair * half:(pair + 1) * half, :] = jnp.where(slab == 0, block[:half], block[half:2 * half])

    basis_ref[:RANK, :RANK] = out_ref[model_layer].astype(F32)
    out_rows = jnp.concatenate(
        [basis_ref[pl.ds(0, RANK // 2, stride=2), :], basis_ref[pl.ds(1, RANK // 2, stride=2), :]], axis=0
    )
    out_t = out_rows.T[:RANK].astype(BF16)
    out_rows = out_rows[:, :RANK].astype(BF16)
    out_twice = jnp.concatenate([out_rows, out_rows], axis=1)
    out_t_twice = jnp.concatenate([out_t, out_t], axis=1)

    in_wide = jnp.concatenate([in_ref[model_layer].astype(F32)] * 4, axis=1)
    in_tall = jnp.concatenate([in_wide] * 4, axis=0)
    in_diag = jnp.where(row == col, in_tall, F32(0.0)).astype(BF16)
    eigen = jnp.concatenate([eigen_ref[model_layer]] * 4, axis=1)

    quads = range(half // 4)
    grids = []
    for quad in quads:
        tops, bottoms = [], []
        for two in range(2):
            at = quad * 4 + two * 2
            a = rows_ref[pl.ds(at, pairs, stride=half), :]
            b = rows_ref[pl.ds(at + 1, pairs, stride=half), :]
            tops.append(jnp.where(low_lanes, a, pltpu.roll(b, RANK, 1)))
            bottoms.append(jnp.where(low_lanes, pltpu.roll(a, RANK, 1), b))
        grids += [jnp.concatenate(tops, axis=1), jnp.concatenate(bottoms, axis=1)]
    right = jnp.dot(jnp.concatenate(grids, axis=0).astype(BF16), in_diag, preferred_element_type=F32)
    middles = [
        jnp.dot(
            out_t_twice, jnp.concatenate(split(right[quad * RANK:(quad + 1) * RANK]), axis=0),
            preferred_element_type=F32,
        )
        for quad in quads
    ]
    scaled = []
    for quad in quads:
        damp = jnp.zeros((1, 4 * RANK), F32)
        for one in range(4):
            block = block_ref[first + quad * 4 + one]
            value = F32(0.0)
            for k in range(BLOCKS):
                value = jnp.where(block == k, damping_ref[k], value)
            damp = jnp.where(lane == one, value, damp)
        scaled.append(middles[quad] / (eigen + damp))
    turned = [
        jnp.dot(out_twice, jnp.concatenate(split(block), axis=0), preferred_element_type=F32) for block in scaled
    ]
    hi, lo = split(jnp.concatenate(turned, axis=0))
    result = lax.dot_general(hi, in_diag, NT, preferred_element_type=F32)
    result = result + lax.dot_general(lo, in_diag, NT, preferred_element_type=F32)
    for quad in quads:
        for two in range(2):
            at = quad * 4 + two * 2
            top = result[quad * RANK:quad * RANK + pairs, two * 128:(two + 1) * 128]
            bottom = result[quad * RANK + pairs:(quad + 1) * RANK, two * 128:(two + 1) * 128]
            turned_ref[pl.ds(at, pairs, stride=half), :] = jnp.where(low_lanes, top, pltpu.roll(bottom, RANK, 1))
            turned_ref[pl.ds(at + 1, pairs, stride=half), :] = jnp.where(low_lanes, pltpu.roll(top, RANK, 1), bottom)

    for pair in range(pairs):
        result_ref[:, pair * 128:(pair + 1) * 128] = turned_ref[pair * half:(pair + 1) * half, :].astype(BF16)


def rotate(query_grads, query_block, layer_slot, out_basis, in_basis, eigen_values, damping):
    half = query_grads.shape[1] // lax.axis_size("slab")
    dim = query_grads.shape[2]
    operands = (query_grads, query_block, damping, layer_slot, out_basis, in_basis, eigen_values)
    homes = (pltpu.VMEM, pltpu.SMEM, pltpu.SMEM, pltpu.SMEM, pltpu.VMEM, pltpu.VMEM, pltpu.VMEM)
    return pl.pallas_call(
        functools.partial(rotate_kernel, half, 1),
        out_shape=jax.ShapeDtypeStruct((half, dim), BF16),
        in_specs=[pl.BlockSpec(memory_space=pltpu.HBM)] * len(operands),
        out_specs=pl.BlockSpec(memory_space=pltpu.VMEM),
        scratch_shapes=[home(x.shape, x.dtype) for home, x in zip(homes, operands)] + [
            pltpu.VMEM((half * (dim // 128 + 1), 128), F32),
            pltpu.VMEM((RANK + 8, 128), F32),
            pltpu.VMEM((half * (dim // 128 + 1), 128), F32),
            pltpu.SemaphoreType.DMA((len(operands),)),
        ],
        compiler_params=pltpu.CompilerParams(vmem_limit_bytes=16 << 20),
        cost_estimate=pl.CostEstimate(flops=8 * half * dim * 256, bytes_accessed=1 << 20, transcendentals=0),
        name="rotate",
    )(*map(in_hbm, operands))


def fetch_kernel(shares, after_ref, store_hbm, store_ref, turned_ref, sems):
    del after_ref
    parts = sems.shape[0]
    rows = store_ref.shape[1] // parts
    copies = [
        pltpu.make_async_copy(
            store_hbm.at[:, pl.ds(k * rows, rows)], store_ref.at[:, pl.ds(k * rows, rows)], sems.at[k]
        )
        for k in range(parts)
    ]
    for copy in copies:
        copy.start()
    for copy in copies:
        copy.wait()
    lay = lax.axis_index("lay")
    for k in range(shares - 1):
        share = turned_ref.shape[2]
        owned = pl.ds(pl.multiple_of(lax.rem(lay + k + 1, shares) * share, share), share)
        turned_ref[k] = store_ref[0, owned, :].T


def fetch(after, store):
    shares = lax.axis_size("lay")
    _, examples, dim = store.shape
    vmem = pl.BlockSpec(memory_space=pltpu.VMEM)
    return pl.pallas_call(
        functools.partial(fetch_kernel, shares),
        out_shape=[
            jax.ShapeDtypeStruct(store.shape, store.dtype),
            jax.ShapeDtypeStruct((shares - 1, dim, examples // shares), store.dtype),
        ],
        in_specs=[vmem, pl.BlockSpec(memory_space=pltpu.HBM)],
        out_specs=[vmem] * 2,
        scratch_shapes=[pltpu.SemaphoreType.DMA((4,))],
        compiler_params=pltpu.CompilerParams(vmem_limit_bytes=24 << 20),
        cost_estimate=pl.CostEstimate(flops=0, bytes_accessed=2 * store.size * 2, transcendentals=0),
        name="fetch",
    )(after, in_hbm(store))


def score_kernel(count, height, share, shares, owners, turned, *refs):
    outs, held = refs[-1 - len(owners):-1], refs[-1]
    pieces, store_ref = refs[:-2 - len(owners)], refs[-2 - len(owners)]
    half = pieces[0].shape[0]
    for k, piece in enumerate(pieces[:count]):
        held[k * height:k * height + half, :] = piece[...]
    column = 0
    for piece in pieces[count:]:
        held[count * height:count * height + half, column:column + piece.shape[1]] = piece[...]
        column += piece.shape[1]
    lay = lax.axis_index("lay")
    for out, owner in zip(outs, owners):
        if not turned:
            rows = pl.ds(pl.multiple_of(lax.rem(lay + owner, shares) * share, share), share)
            block = lax.dot_general(held[...], store_ref[0, rows, :], NT, preferred_element_type=F32)
        else:
            block = jnp.dot(held[...], store_ref[owner - 1], preferred_element_type=F32)
        for j in range(out.shape[0] // half):
            out[j * half:(j + 1) * half, :] = block[j * height:j * height + half].astype(out.dtype)


def score(pieces, parts, store, owners, turned=False):
    half = (pieces + parts)[0].shape[0]
    dim = pieces[0].shape[1] if pieces else sum(part.shape[1] for part in parts)
    shares = lax.axis_size("lay")
    share = store.shape[2] if turned else store.shape[1] // shares
    whole = len(pieces) + (1 if parts else 0)
    height = -(-half // 16) * 16
    vmem = pl.BlockSpec(memory_space=pltpu.VMEM)
    return pl.pallas_call(
        functools.partial(score_kernel, len(pieces), height, share, shares, tuple(owners), turned),
        out_shape=[jax.ShapeDtypeStruct((whole * half, share), BF16 if owner else F32) for owner in owners],
        in_specs=[vmem] * (len(pieces) + len(parts) + 1),
        out_specs=[vmem] * len(owners),
        scratch_shapes=[pltpu.VMEM((whole * height, dim), BF16)],
        compiler_params=pltpu.CompilerParams(vmem_limit_bytes=24 << 20),
        cost_estimate=pl.CostEstimate(
            flops=2 * 256 * share * len(owners) * dim, bytes_accessed=1 << 20, transcendentals=0
        ),
        name="score",
    )(*pieces, *parts, store)


def swap_layers(sends):
    shares = lax.axis_size("lay")
    return [
        lax.ppermute(send, "lay", [(i, (i + k + 1) % shares) for i in range(shares)])
        for k, send in enumerate(sends)
    ]


def finish_kernel(half, members, sizes, *refs):
    out_ref = refs[-1]
    refs = refs[:-1]
    count = len(sizes)
    each = len(refs) // count
    slab, ex = lax.axis_index("slab"), lax.axis_index("ex")
    place = jnp.where(slab == 0, ex, 2 * members - 1 - ex)
    at = 0
    for k, size in enumerate(sizes):
        keep, got = refs[k * each], refs[k * each + 1:(k + 1) * each]
        for j in range(size):
            rows = slice(j * half, (j + 1) * half)
            total = keep[rows, :]
            for g in got:
                total = total + g[rows, :].astype(F32)
            distance = (at + 1) // 2
            hops = 2 * members - distance if at % 2 == 1 else distance
            source = lax.rem(place + hops, 2 * members)
            block = jnp.where(source < members, 2 * source, 2 * (2 * members - 1 - source) + 1)
            out_ref[pl.ds(pl.multiple_of(block * half, 8), half), :] = total
            at += 1


def finish(half, parts):
    members = lax.axis_size("ex")
    vmem = pl.BlockSpec(memory_space=pltpu.VMEM)
    flat = [array for keep, got in parts for array in [keep, *got]]
    sizes = [keep.shape[0] // half for keep, _ in parts]
    return pl.pallas_call(
        functools.partial(finish_kernel, half, members, sizes),
        out_shape=jax.ShapeDtypeStruct((2 * members * half, flat[0].shape[1]), F32),
        in_specs=[vmem] * len(flat),
        out_specs=vmem,
        compiler_params=pltpu.CompilerParams(vmem_limit_bytes=16 << 20),
        name="finish",
    )(*flat)


def local(
    store_grads, query_grads, query_block, layer_slot, out_basis, in_basis, eigen_values, damping
):
    members = lax.axis_size("ex")
    ring = list(range(members)) + [members + i for i in reversed(range(members))]

    def hop(piece, steps):
        return lax.ppermute(piece, RING, [(a, ring[(i + steps) % len(ring)]) for i, a in enumerate(ring)])

    own = rotate(query_grads, query_block, layer_slot, out_basis, in_basis, eigen_values, damping)
    store, turned = fetch(own, store_grads)
    half, dim = own.shape
    others = range(1, lax.axis_size("lay"))
    one = two = own
    batch, sums, hidden = [own], [], [store, turned]
    for step in range(1, members):
        if step == members - 1:
            cut = dim // 8 * 5 // 128 * 128
            parts = [one[:, :cut], two[:, cut:]]
        one, two = hop(one, 1), hop(two, -1)
        if step == members - 1:
            parts = [hop(parts[0], 2), hop(parts[1], -2)]
        if step < members - 1:
            one, hidden = lax.optimization_barrier((one, hidden))
        if step == 1:
            store, turned = hidden
        elif hidden:
            keep, *sends = hidden
            sums.append((keep, swap_layers(sends)))
        hidden = []
        batch += [one, two]
        if len(batch) >= 5 and step < members - 1:
            hidden = score(batch, [], store, [0, *others])
            batch = []
    sends = score(batch, [], turned, others, True)
    near = swap_layers(sends)
    parts, _ = lax.optimization_barrier((parts, sends))
    far = swap_layers(score([], parts, turned, others, True))
    (keep,) = score(batch, parts, store, [0])
    rows = len(batch) * half
    sums += [(keep[:rows], near), (keep[rows:], far)]
    return finish(half, sums).T


def solution(mesh):
    return jax.shard_map(
        local,
        mesh=mesh,
        in_specs=(
            P("lay", ("slab", "ex"), None),
            P("lay", ("pb", "ex"), None),
            P(),
            P(),
            P(),
            P(),
            P(),
            P(),
        ),
        out_specs=P(("slab", "ex", "lay"), "pb"),
        check_vma=False,
    )
```

```python
import functools

import jax
import jax.numpy as jnp
from jax import lax
from jax.experimental import pallas as pl
from jax.experimental.pallas import tpu as pltpu
from jax.sharding import PartitionSpec as P

RANK = 64
BLOCKS = 4
F32 = jnp.float32
BF16 = jnp.bfloat16
NT = (((1,), (1,)), ((), ()))
RING = ("slab", "ex")


def in_hbm(x):
    return pltpu.with_memory_space_constraint(x, pltpu.HBM)


def split(x):
    hi = x.astype(BF16)
    return hi, (x - hi.astype(F32)).astype(BF16)


def rotate_kernel(
    half, lay_slots, query_hbm, block_hbm, damping_hbm, slot_hbm, out_hbm, in_hbm, eigen_hbm,
    result_ref, query_ref, block_ref, damping_ref, slot_ref, out_ref, in_ref, eigen_ref,
    rows_ref, basis_ref, turned_ref, sems,
):
    pairs = RANK * RANK // 128
    local = query_ref.shape[1]
    copies = [
        pltpu.make_async_copy(source, target, sems.at[k])
        for k, (source, target) in enumerate([
            (slot_hbm, slot_ref), (query_hbm, query_ref), (block_hbm, block_ref), (damping_hbm, damping_ref),
            (out_hbm, out_ref), (in_hbm, in_ref), (eigen_hbm, eigen_ref),
        ])
    ]
    for copy in copies:
        copy.start()
    slab = lax.axis_index("slab")
    first = (lax.axis_index("pb") * lax.axis_size("ex") + lax.axis_index("ex")) * local + slab * half
    low_lanes = lax.broadcasted_iota(jnp.int32, (RANK // 2, 128), 1) < RANK
    row = lax.broadcasted_iota(jnp.int32, (4 * RANK, 4 * RANK), 0) // RANK
    col = lax.broadcasted_iota(jnp.int32, (4 * RANK, 4 * RANK), 1) // RANK
    lane = lax.broadcasted_iota(jnp.int32, (1, 4 * RANK), 1) // RANK
    for copy in copies:
        copy.wait()
    model_layer = slot_ref[lax.axis_index("lay") * lay_slots]

    for pair in range(pairs):
        block = query_ref[0, :, pair * 128:(pair + 1) * 128].astype(F32)
        rows_ref[pair * half:(pair + 1) * half, :] = jnp.where(slab == 0, block[:half], block[half:2 * half])

    basis_ref[:RANK, :RANK] = out_ref[model_layer].astype(F32)
    out_rows = jnp.concatenate(
        [basis_ref[pl.ds(0, RANK // 2, stride=2), :], basis_ref[pl.ds(1, RANK // 2, stride=2), :]], axis=0
    )
    out_t = out_rows.T[:RANK].astype(BF16)
    out_rows = out_rows[:, :RANK].astype(BF16)
    out_twice = jnp.concatenate([out_rows, out_rows], axis=1)
    out_t_twice = jnp.concatenate([out_t, out_t], axis=1)

    in_wide = jnp.concatenate([in_ref[model_layer].astype(F32)] * 4, axis=1)
    in_tall = jnp.concatenate([in_wide] * 4, axis=0)
    in_diag = jnp.where(row == col, in_tall, F32(0.0)).astype(BF16)
    in_diag_t = jnp.where(row == col, in_tall.T, F32(0.0)).astype(BF16)
    eigen = jnp.concatenate([eigen_ref[model_layer]] * 4, axis=1)

    quads = range(half // 4)
    grids = []
    for quad in quads:
        tops, bottoms = [], []
        for two in range(2):
            at = quad * 4 + two * 2
            a = rows_ref[pl.ds(at, pairs, stride=half), :]
            b = rows_ref[pl.ds(at + 1, pairs, stride=half), :]
            tops.append(jnp.where(low_lanes, a, pltpu.roll(b, RANK, 1)))
            bottoms.append(jnp.where(low_lanes, pltpu.roll(a, RANK, 1), b))
        grids += [jnp.concatenate(tops, axis=1), jnp.concatenate(bottoms, axis=1)]
    right = jnp.dot(jnp.concatenate(grids, axis=0).astype(BF16), in_diag, preferred_element_type=F32)
    middles = [
        jnp.dot(
            out_t_twice, jnp.concatenate(split(right[quad * RANK:(quad + 1) * RANK]), axis=0),
            preferred_element_type=F32,
        )
        for quad in quads
    ]
    scaled = []
    for quad in quads:
        damp = jnp.zeros((1, 4 * RANK), F32)
        for one in range(4):
            block = block_ref[first + quad * 4 + one]
            value = F32(0.0)
            for k in range(BLOCKS):
                value = jnp.where(block == k, damping_ref[k], value)
            damp = jnp.where(lane == one, value, damp)
        scaled.append(middles[quad] / (eigen + damp))
    turned = [
        jnp.dot(out_twice, jnp.concatenate(split(block), axis=0), preferred_element_type=F32) for block in scaled
    ]
    hi, lo = split(jnp.concatenate(turned, axis=0))
    result = jnp.dot(hi, in_diag_t, preferred_element_type=F32)
    result = result + jnp.dot(lo, in_diag_t, preferred_element_type=F32)
    for quad in quads:
        for two in range(2):
            at = quad * 4 + two * 2
            top = result[quad * RANK:quad * RANK + pairs, two * 128:(two + 1) * 128]
            bottom = result[quad * RANK + pairs:(quad + 1) * RANK, two * 128:(two + 1) * 128]
            turned_ref[pl.ds(at, pairs, stride=half), :] = jnp.where(low_lanes, top, pltpu.roll(bottom, RANK, 1))
            turned_ref[pl.ds(at + 1, pairs, stride=half), :] = jnp.where(low_lanes, pltpu.roll(top, RANK, 1), bottom)

    for pair in range(pairs):
        result_ref[:, pair * 128:(pair + 1) * 128] = turned_ref[pair * half:(pair + 1) * half, :].astype(BF16)


def rotate(query_grads, query_block, layer_slot, out_basis, in_basis, eigen_values, damping):
    half = query_grads.shape[1] // lax.axis_size("slab")
    dim = query_grads.shape[2]
    operands = (query_grads, query_block, damping, layer_slot, out_basis, in_basis, eigen_values)
    homes = (pltpu.VMEM, pltpu.SMEM, pltpu.SMEM, pltpu.SMEM, pltpu.VMEM, pltpu.VMEM, pltpu.VMEM)
    return pl.pallas_call(
        functools.partial(rotate_kernel, half, 1),
        out_shape=jax.ShapeDtypeStruct((half, dim), BF16),
        in_specs=[pl.BlockSpec(memory_space=pltpu.HBM)] * len(operands),
        out_specs=pl.BlockSpec(memory_space=pltpu.VMEM),
        scratch_shapes=[home(x.shape, x.dtype) for home, x in zip(homes, operands)] + [
            pltpu.VMEM((half * (dim // 128 + 1), 128), F32),
            pltpu.VMEM((RANK + 8, 128), F32),
            pltpu.VMEM((half * (dim // 128 + 1), 128), F32),
            pltpu.SemaphoreType.DMA((len(operands),)),
        ],
        compiler_params=pltpu.CompilerParams(vmem_limit_bytes=16 << 20),
        cost_estimate=pl.CostEstimate(flops=8 * half * dim * 256, bytes_accessed=1 << 20, transcendentals=0),
        name="rotate",
    )(*map(in_hbm, operands))


def fetch_kernel(shares, after_ref, store_hbm, store_ref, turned_ref, sems):
    del after_ref
    parts = sems.shape[0]
    rows = store_ref.shape[1] // parts
    copies = [
        pltpu.make_async_copy(
            store_hbm.at[:, pl.ds(k * rows, rows)], store_ref.at[:, pl.ds(k * rows, rows)], sems.at[k]
        )
        for k in range(parts)
    ]
    for copy in copies:
        copy.start()
    for copy in copies:
        copy.wait()
    lay = lax.axis_index("lay")
    for k in range(shares - 1):
        share = turned_ref.shape[2]
        owned = pl.ds(pl.multiple_of(lax.rem(lay + k + 1, shares) * share, share), share)
        turned_ref[k] = store_ref[0, owned, :].T


def fetch(after, store):
    shares = lax.axis_size("lay")
    _, examples, dim = store.shape
    vmem = pl.BlockSpec(memory_space=pltpu.VMEM)
    return pl.pallas_call(
        functools.partial(fetch_kernel, shares),
        out_shape=[
            jax.ShapeDtypeStruct(store.shape, store.dtype),
            jax.ShapeDtypeStruct((shares - 1, dim, examples // shares), store.dtype),
        ],
        in_specs=[vmem, pl.BlockSpec(memory_space=pltpu.HBM)],
        out_specs=[vmem] * 2,
        scratch_shapes=[pltpu.SemaphoreType.DMA((4,))],
        compiler_params=pltpu.CompilerParams(vmem_limit_bytes=24 << 20),
        cost_estimate=pl.CostEstimate(flops=0, bytes_accessed=2 * store.size * 2, transcendentals=0),
        name="fetch",
    )(after, in_hbm(store))


def score_kernel(count, height, share, shares, owners, turned, *refs):
    outs, held = refs[-1 - len(owners):-1], refs[-1]
    pieces, store_ref = refs[:-2 - len(owners)], refs[-2 - len(owners)]
    half = pieces[0].shape[0]
    for k, piece in enumerate(pieces[:count]):
        held[k * height:k * height + half, :] = piece[...]
    column = 0
    for piece in pieces[count:]:
        held[count * height:count * height + half, column:column + piece.shape[1]] = piece[...]
        column += piece.shape[1]
    lay = lax.axis_index("lay")
    for out, owner in zip(outs, owners):
        if not turned:
            rows = pl.ds(pl.multiple_of(lax.rem(lay + owner, shares) * share, share), share)
            block = lax.dot_general(held[...], store_ref[0, rows, :], NT, preferred_element_type=F32)
        else:
            block = jnp.dot(held[...], store_ref[owner - 1], preferred_element_type=F32)
        for j in range(out.shape[0] // half):
            out[j * half:(j + 1) * half, :] = block[j * height:j * height + half].astype(out.dtype)


def score(pieces, parts, store, owners, turned=False):
    half = (pieces + parts)[0].shape[0]
    dim = pieces[0].shape[1] if pieces else sum(part.shape[1] for part in parts)
    shares = lax.axis_size("lay")
    share = store.shape[2] if turned else store.shape[1] // shares
    whole = len(pieces) + (1 if parts else 0)
    height = -(-half // 16) * 16
    vmem = pl.BlockSpec(memory_space=pltpu.VMEM)
    return pl.pallas_call(
        functools.partial(score_kernel, len(pieces), height, share, shares, tuple(owners), turned),
        out_shape=[jax.ShapeDtypeStruct((whole * half, share), BF16 if owner else F32) for owner in owners],
        in_specs=[vmem] * (len(pieces) + len(parts) + 1),
        out_specs=[vmem] * len(owners),
        scratch_shapes=[pltpu.VMEM((whole * height, dim), BF16)],
        compiler_params=pltpu.CompilerParams(vmem_limit_bytes=24 << 20),
        cost_estimate=pl.CostEstimate(
            flops=2 * 256 * share * len(owners) * dim, bytes_accessed=1 << 20, transcendentals=0
        ),
        name="score",
    )(*pieces, *parts, store)


def swap_layers(sends):
    shares = lax.axis_size("lay")
    return [
        lax.ppermute(send, "lay", [(i, (i + k + 1) % shares) for i in range(shares)])
        for k, send in enumerate(sends)
    ]


def finish_kernel(half, members, sizes, *refs):
    out_ref = refs[-1]
    refs = refs[:-1]
    count = len(sizes)
    each = len(refs) // count
    slab, ex = lax.axis_index("slab"), lax.axis_index("ex")
    place = jnp.where(slab == 0, ex, 2 * members - 1 - ex)
    at = 0
    for k, size in enumerate(sizes):
        keep, got = refs[k * each], refs[k * each + 1:(k + 1) * each]
        for j in range(size):
            rows = slice(j * half, (j + 1) * half)
            total = keep[rows, :]
            for g in got:
                total = total + g[rows, :].astype(F32)
            distance = (at + 1) // 2
            hops = 2 * members - distance if at % 2 == 1 else distance
            source = lax.rem(place + hops, 2 * members)
            block = jnp.where(source < members, 2 * source, 2 * (2 * members - 1 - source) + 1)
            out_ref[pl.ds(pl.multiple_of(block * half, 8), half), :] = total
            at += 1


def finish(half, parts):
    members = lax.axis_size("ex")
    vmem = pl.BlockSpec(memory_space=pltpu.VMEM)
    flat = [array for keep, got in parts for array in [keep, *got]]
    sizes = [keep.shape[0] // half for keep, _ in parts]
    return pl.pallas_call(
        functools.partial(finish_kernel, half, members, sizes),
        out_shape=jax.ShapeDtypeStruct((2 * members * half, flat[0].shape[1]), F32),
        in_specs=[vmem] * len(flat),
        out_specs=vmem,
        compiler_params=pltpu.CompilerParams(vmem_limit_bytes=16 << 20),
        name="finish",
    )(*flat)


def local(
    store_grads, query_grads, query_block, layer_slot, out_basis, in_basis, eigen_values, damping
):
    members = lax.axis_size("ex")
    ring = list(range(members)) + [members + i for i in reversed(range(members))]

    def hop(piece, steps):
        return lax.ppermute(piece, RING, [(a, ring[(i + steps) % len(ring)]) for i, a in enumerate(ring)])

    own = rotate(query_grads, query_block, layer_slot, out_basis, in_basis, eigen_values, damping)
    store, turned = fetch(own, store_grads)
    half, dim = own.shape
    others = range(1, lax.axis_size("lay"))
    one = two = own
    batch, sums = [own], []
    for step in range(1, members):
        if step == members - 1:
            cut = dim // 8 * 5 // 128 * 128
            parts = [one[:, :cut], two[:, cut:]]
        one, two = hop(one, 1), hop(two, -1)
        if step == members - 1:
            parts = [hop(parts[0], 2), hop(parts[1], -2)]
        if step == 1:
            one, store, turned = lax.optimization_barrier((one, store, turned))
        elif len(batch) >= 7:
            keep, *sends = score(batch, [], store, [0, *others])
            got = swap_layers(sends)
            if step < members - 1:
                one, _ = lax.optimization_barrier((one, sends))
            sums.append((keep, got))
            batch = []
        batch += [one, two]
    sends = score(batch, [], turned, others, True)
    near = swap_layers(sends)
    parts, _ = lax.optimization_barrier((parts, sends))
    far = swap_layers(score([], parts, turned, others, True))
    (keep,) = score(batch, parts, store, [0])
    rows = len(batch) * half
    sums += [(keep[:rows], near), (keep[rows:], far)]
    return finish(half, sums).T


def solution(mesh):
    return jax.shard_map(
        local,
        mesh=mesh,
        in_specs=(
            P("lay", ("slab", "ex"), None),
            P("lay", ("pb", "ex"), None),
            P(),
            P(),
            P(),
            P(),
            P(),
            P(),
        ),
        out_specs=P(("slab", "ex", "lay"), "pb"),
        check_vma=False,
    )
```

```python
import functools

import jax
import jax.numpy as jnp
from jax import lax
from jax.experimental import pallas as pl
from jax.experimental.pallas import tpu as pltpu
from jax.sharding import PartitionSpec as P

RANK = 64
BLOCKS = 4
F32 = jnp.float32
BF16 = jnp.bfloat16
NT = (((1,), (1,)), ((), ()))
RING = ("slab", "ex")


def in_hbm(x):
    return pltpu.with_memory_space_constraint(x, pltpu.HBM)


def split(x):
    hi = x.astype(BF16)
    return hi, (x - hi.astype(F32)).astype(BF16)


def rotate_kernel(
    half, lay_slots, query_hbm, block_hbm, damping_hbm, slot_hbm, out_hbm, in_hbm, eigen_hbm,
    result_ref, query_ref, block_ref, damping_ref, slot_ref, out_ref, in_ref, eigen_ref,
    rows_ref, basis_ref, turned_ref, sems,
):
    pairs = RANK * RANK // 128
    local = query_ref.shape[1]
    copies = [
        pltpu.make_async_copy(source, target, sems.at[k])
        for k, (source, target) in enumerate([
            (slot_hbm, slot_ref), (query_hbm, query_ref), (block_hbm, block_ref), (damping_hbm, damping_ref),
            (out_hbm, out_ref), (in_hbm, in_ref), (eigen_hbm, eigen_ref),
        ])
    ]
    for copy in copies:
        copy.start()
    slab = lax.axis_index("slab")
    first = (lax.axis_index("pb") * lax.axis_size("ex") + lax.axis_index("ex")) * local + slab * half
    low_lanes = lax.broadcasted_iota(jnp.int32, (RANK // 2, 128), 1) < RANK
    row = lax.broadcasted_iota(jnp.int32, (4 * RANK, 4 * RANK), 0) // RANK
    col = lax.broadcasted_iota(jnp.int32, (4 * RANK, 4 * RANK), 1) // RANK
    lane = lax.broadcasted_iota(jnp.int32, (1, 4 * RANK), 1) // RANK
    for copy in copies:
        copy.wait()
    model_layer = slot_ref[lax.axis_index("lay") * lay_slots]

    for pair in range(pairs):
        block = query_ref[0, :, pair * 128:(pair + 1) * 128].astype(F32)
        rows_ref[pair * half:(pair + 1) * half, :] = jnp.where(slab == 0, block[:half], block[half:2 * half])

    basis_ref[:RANK, :RANK] = out_ref[model_layer].astype(F32)
    out_rows = jnp.concatenate(
        [basis_ref[pl.ds(0, RANK // 2, stride=2), :], basis_ref[pl.ds(1, RANK // 2, stride=2), :]], axis=0
    )
    out_t = out_rows.T[:RANK].astype(BF16)
    out_rows = out_rows[:, :RANK].astype(BF16)
    out_twice = jnp.concatenate([out_rows, out_rows], axis=1)
    out_t_twice = jnp.concatenate([out_t, out_t], axis=1)

    in_wide = jnp.concatenate([in_ref[model_layer].astype(F32)] * 4, axis=1)
    in_tall = jnp.concatenate([in_wide] * 4, axis=0)
    in_diag = jnp.where(row == col, in_tall, F32(0.0)).astype(BF16)
    in_diag_t = jnp.where(row == col, in_tall.T, F32(0.0)).astype(BF16)
    eigen = jnp.concatenate([eigen_ref[model_layer]] * 4, axis=1)

    quads = range(half // 4)
    grids = []
    for quad in quads:
        tops, bottoms = [], []
        for two in range(2):
            at = quad * 4 + two * 2
            a = rows_ref[pl.ds(at, pairs, stride=half), :]
            b = rows_ref[pl.ds(at + 1, pairs, stride=half), :]
            tops.append(jnp.where(low_lanes, a, pltpu.roll(b, RANK, 1)))
            bottoms.append(jnp.where(low_lanes, pltpu.roll(a, RANK, 1), b))
        grids += [jnp.concatenate(tops, axis=1), jnp.concatenate(bottoms, axis=1)]
    right = jnp.dot(jnp.concatenate(grids, axis=0).astype(BF16), in_diag, preferred_element_type=F32)
    middles = [
        jnp.dot(
            out_t_twice, jnp.concatenate(split(right[quad * RANK:(quad + 1) * RANK]), axis=0),
            preferred_element_type=F32,
        )
        for quad in quads
    ]
    scaled = []
    for quad in quads:
        damp = jnp.zeros((1, 4 * RANK), F32)
        for one in range(4):
            block = block_ref[first + quad * 4 + one]
            value = F32(0.0)
            for k in range(BLOCKS):
                value = jnp.where(block == k, damping_ref[k], value)
            damp = jnp.where(lane == one, value, damp)
        scaled.append(middles[quad] / (eigen + damp))
    turned = [
        jnp.dot(out_twice, jnp.concatenate(split(block), axis=0), preferred_element_type=F32) for block in scaled
    ]
    hi, lo = split(jnp.concatenate(turned, axis=0))
    result = jnp.dot(hi, in_diag_t, preferred_element_type=F32)
    result = result + jnp.dot(lo, in_diag_t, preferred_element_type=F32)
    for quad in quads:
        for two in range(2):
            at = quad * 4 + two * 2
            top = result[quad * RANK:quad * RANK + pairs, two * 128:(two + 1) * 128]
            bottom = result[quad * RANK + pairs:(quad + 1) * RANK, two * 128:(two + 1) * 128]
            turned_ref[pl.ds(at, pairs, stride=half), :] = jnp.where(low_lanes, top, pltpu.roll(bottom, RANK, 1))
            turned_ref[pl.ds(at + 1, pairs, stride=half), :] = jnp.where(low_lanes, pltpu.roll(top, RANK, 1), bottom)

    for pair in range(pairs):
        result_ref[:, pair * 128:(pair + 1) * 128] = turned_ref[pair * half:(pair + 1) * half, :].astype(BF16)


def rotate(query_grads, query_block, layer_slot, out_basis, in_basis, eigen_values, damping):
    half = query_grads.shape[1] // lax.axis_size("slab")
    dim = query_grads.shape[2]
    operands = (query_grads, query_block, damping, layer_slot, out_basis, in_basis, eigen_values)
    homes = (pltpu.VMEM, pltpu.SMEM, pltpu.SMEM, pltpu.SMEM, pltpu.VMEM, pltpu.VMEM, pltpu.VMEM)
    return pl.pallas_call(
        functools.partial(rotate_kernel, half, 1),
        out_shape=jax.ShapeDtypeStruct((half, dim), BF16),
        in_specs=[pl.BlockSpec(memory_space=pltpu.HBM)] * len(operands),
        out_specs=pl.BlockSpec(memory_space=pltpu.VMEM),
        scratch_shapes=[home(x.shape, x.dtype) for home, x in zip(homes, operands)] + [
            pltpu.VMEM((half * (dim // 128 + 1), 128), F32),
            pltpu.VMEM((RANK + 8, 128), F32),
            pltpu.VMEM((half * (dim // 128 + 1), 128), F32),
            pltpu.SemaphoreType.DMA((len(operands),)),
        ],
        compiler_params=pltpu.CompilerParams(vmem_limit_bytes=16 << 20),
        cost_estimate=pl.CostEstimate(flops=8 * half * dim * 256, bytes_accessed=1 << 20, transcendentals=0),
        name="rotate",
    )(*map(in_hbm, operands))


def fetch_kernel(shares, after_ref, store_hbm, store_ref, turned_ref, sems):
    del after_ref
    parts = sems.shape[0]
    rows = store_ref.shape[1] // parts
    copies = [
        pltpu.make_async_copy(
            store_hbm.at[:, pl.ds(k * rows, rows)], store_ref.at[:, pl.ds(k * rows, rows)], sems.at[k]
        )
        for k in range(parts)
    ]
    for copy in copies:
        copy.start()
    for copy in copies:
        copy.wait()
    lay = lax.axis_index("lay")
    for k in range(shares - 1):
        share = turned_ref.shape[2]
        owned = pl.ds(pl.multiple_of(lax.rem(lay + k + 1, shares) * share, share), share)
        turned_ref[k] = store_ref[0, owned, :].T


def fetch(after, store):
    shares = lax.axis_size("lay")
    _, examples, dim = store.shape
    vmem = pl.BlockSpec(memory_space=pltpu.VMEM)
    return pl.pallas_call(
        functools.partial(fetch_kernel, shares),
        out_shape=[
            jax.ShapeDtypeStruct(store.shape, store.dtype),
            jax.ShapeDtypeStruct((shares - 1, dim, examples // shares), store.dtype),
        ],
        in_specs=[vmem, pl.BlockSpec(memory_space=pltpu.HBM)],
        out_specs=[vmem] * 2,
        scratch_shapes=[pltpu.SemaphoreType.DMA((4,))],
        compiler_params=pltpu.CompilerParams(vmem_limit_bytes=24 << 20),
        cost_estimate=pl.CostEstimate(flops=0, bytes_accessed=2 * store.size * 2, transcendentals=0),
        name="fetch",
    )(after, in_hbm(store))


def score_kernel(count, height, share, shares, owners, turned, *refs):
    outs, held = refs[-1 - len(owners):-1], refs[-1]
    pieces, store_ref = refs[:-2 - len(owners)], refs[-2 - len(owners)]
    half = pieces[0].shape[0]
    for k, piece in enumerate(pieces[:count]):
        held[k * height:k * height + half, :] = piece[...]
    column = 0
    for piece in pieces[count:]:
        held[count * height:count * height + half, column:column + piece.shape[1]] = piece[...]
        column += piece.shape[1]
    lay = lax.axis_index("lay")
    for out, owner in zip(outs, owners):
        if not turned:
            rows = pl.ds(pl.multiple_of(lax.rem(lay + owner, shares) * share, share), share)
            block = lax.dot_general(held[...], store_ref[0, rows, :], NT, preferred_element_type=F32)
        else:
            block = jnp.dot(held[...], store_ref[owner - 1], preferred_element_type=F32)
        for j in range(out.shape[0] // half):
            out[j * half:(j + 1) * half, :] = block[j * height:j * height + half].astype(out.dtype)


def score(pieces, parts, store, owners, turned=False):
    half = (pieces + parts)[0].shape[0]
    dim = pieces[0].shape[1] if pieces else sum(part.shape[1] for part in parts)
    shares = lax.axis_size("lay")
    share = store.shape[2] if turned else store.shape[1] // shares
    whole = len(pieces) + (1 if parts else 0)
    height = -(-half // 16) * 16
    vmem = pl.BlockSpec(memory_space=pltpu.VMEM)
    return pl.pallas_call(
        functools.partial(score_kernel, len(pieces), height, share, shares, tuple(owners), turned),
        out_shape=[jax.ShapeDtypeStruct((whole * half, share), BF16 if owner else F32) for owner in owners],
        in_specs=[vmem] * (len(pieces) + len(parts) + 1),
        out_specs=[vmem] * len(owners),
        scratch_shapes=[pltpu.VMEM((whole * height, dim), BF16)],
        compiler_params=pltpu.CompilerParams(vmem_limit_bytes=24 << 20),
        cost_estimate=pl.CostEstimate(
            flops=2 * 256 * share * len(owners) * dim, bytes_accessed=1 << 20, transcendentals=0
        ),
        name="score",
    )(*pieces, *parts, store)


def swap_layers(sends):
    shares = lax.axis_size("lay")
    return [
        lax.ppermute(send, "lay", [(i, (i + k + 1) % shares) for i in range(shares)])
        for k, send in enumerate(sends)
    ]


def finish_kernel(half, members, sizes, first, rows_ref, sems, out_hbm, *refs):
    count = len(sizes)
    each = len(refs) // count
    slab, ex = lax.axis_index("slab"), lax.axis_index("ex")
    place = jnp.where(slab == 0, ex, 2 * members - 1 - ex)
    at, copies = first, []
    for k, size in enumerate(sizes):
        keep, got = refs[k * each], refs[k * each + 1:(k + 1) * each]
        for j in range(size):
            rows = slice(j * half, (j + 1) * half)
            total = keep[rows, :]
            for g in got:
                total = total + g[rows, :].astype(F32)
            distance = (at + 1) // 2
            hops = 2 * members - distance if at % 2 == 1 else distance
            source = lax.rem(place + hops, 2 * members)
            block = jnp.where(source < members, 2 * source, 2 * (2 * members - 1 - source) + 1)
            here = slice((at - first) * half, (at - first + 1) * half)
            rows_ref[here, :] = total
            copies.append(pltpu.make_async_copy(
                rows_ref.at[here, :], out_hbm.at[pl.ds(pl.multiple_of(block * half, 8), half), :], sems.at[at - first]
            ))
            copies[-1].start()
            at += 1
    for copy in copies:
        copy.wait()


def finish(half, sums, first=0, before=None):
    members = lax.axis_size("ex")
    vmem, hbm = pl.BlockSpec(memory_space=pltpu.VMEM), pl.BlockSpec(memory_space=pltpu.HBM)
    flat = [array for keep, got in sums for array in [keep, *got]]
    sizes = [keep.shape[0] // half for keep, _ in sums]
    share = flat[0].shape[1]
    ahead = [] if before is None else [before]

    def kernel(*refs):
        out_hbm, rows_ref, sems = refs[-3:]
        finish_kernel(half, members, sizes, first, rows_ref, sems, out_hbm, *refs[len(ahead):-3])

    return pl.pallas_call(
        kernel,
        out_shape=jax.ShapeDtypeStruct((2 * members * half, share), F32),
        in_specs=[hbm] * len(ahead) + [vmem] * len(flat),
        out_specs=hbm,
        input_output_aliases={0: 0} if ahead else {},
        scratch_shapes=[pltpu.VMEM((sum(sizes) * half, share), F32), pltpu.SemaphoreType.DMA((sum(sizes),))],
        compiler_params=pltpu.CompilerParams(vmem_limit_bytes=16 << 20),
        cost_estimate=pl.CostEstimate(flops=0, bytes_accessed=1 << 20, transcendentals=0),
        name="finish",
    )(*ahead, *flat)


def local(
    store_grads, query_grads, query_block, layer_slot, out_basis, in_basis, eigen_values, damping
):
    members = lax.axis_size("ex")
    ring = list(range(members)) + [members + i for i in reversed(range(members))]

    def hop(piece, steps):
        return lax.ppermute(piece, RING, [(a, ring[(i + steps) % len(ring)]) for i, a in enumerate(ring)])

    own = rotate(query_grads, query_block, layer_slot, out_basis, in_basis, eigen_values, damping)
    store, turned = fetch(own, store_grads)
    half, dim = own.shape
    others = range(1, lax.axis_size("lay"))
    one = two = own
    batch, sums = [own], []
    for step in range(1, members):
        if step == members - 1:
            cut = dim // 8 * 5 // 128 * 128
            parts = [one[:, :cut], two[:, cut:]]
        one, two = hop(one, 1), hop(two, -1)
        if step == members - 1:
            parts = [hop(parts[0], 2), hop(parts[1], -2)]
        if step == 1:
            one, store, turned = lax.optimization_barrier((one, store, turned))
        elif len(batch) >= 7:
            keep, *sends = score(batch, [], store, [0, *others])
            got = swap_layers(sends)
            if step < members - 1:
                one, _ = lax.optimization_barrier((one, sends))
            sums.append((keep, got))
            batch = []
        batch += [one, two]
    sends = score(batch, [], turned, others, True)
    near = swap_layers(sends)
    parts, _ = lax.optimization_barrier((parts, sends))
    far = swap_layers(score([], parts, turned, others, True))
    (keep,) = score(batch, parts, store, [0])
    rows = len(batch) * half
    sums.append((keep[:rows], near))
    scores = finish(half, sums)
    return finish(half, [(keep[rows:], far)], 2 * members - 1, scores).T


def solution(mesh):
    return jax.shard_map(
        local,
        mesh=mesh,
        in_specs=(
            P("lay", ("slab", "ex"), None),
            P("lay", ("pb", "ex"), None),
            P(),
            P(),
            P(),
            P(),
            P(),
            P(),
        ),
        out_specs=P(("slab", "ex", "lay"), "pb"),
        check_vma=False,
    )
```

```python
import functools

import jax
import jax.numpy as jnp
from jax import lax
from jax.experimental import pallas as pl
from jax.experimental.pallas import tpu as pltpu
from jax.sharding import PartitionSpec as P

RANK = 64
BLOCKS = 4
F32 = jnp.float32
BF16 = jnp.bfloat16
NT = (((1,), (1,)), ((), ()))
RING = ("slab", "ex")


def in_hbm(x):
    return pltpu.with_memory_space_constraint(x, pltpu.HBM)


def split(x):
    hi = x.astype(BF16)
    return hi, (x - hi.astype(F32)).astype(BF16)


def rotate_kernel(
    half, lay_slots, query_hbm, block_hbm, damping_hbm, slot_hbm, out_hbm, in_hbm, eigen_hbm,
    result_ref, query_ref, block_ref, damping_ref, slot_ref, out_ref, in_ref, eigen_ref,
    rows_ref, basis_ref, turned_ref, sems,
):
    pairs = RANK * RANK // 128
    local, span = query_hbm.shape[1], query_ref.shape[1]
    slab = lax.axis_index("slab")
    begin = pl.multiple_of(slab * (local - span), 16)
    later = half - (local - span)
    copies = [
        pltpu.make_async_copy(source, target, sems.at[k])
        for k, (source, target) in enumerate([
            (slot_hbm, slot_ref), (query_hbm.at[:, pl.ds(begin, span), :], query_ref), (block_hbm, block_ref), (damping_hbm, damping_ref),
            (out_hbm, out_ref), (in_hbm, in_ref), (eigen_hbm, eigen_ref),
        ])
    ]
    for copy in copies:
        copy.start()
    first = (lax.axis_index("pb") * lax.axis_size("ex") + lax.axis_index("ex")) * local + slab * half
    low_lanes = lax.broadcasted_iota(jnp.int32, (RANK // 2, 128), 1) < RANK
    row = lax.broadcasted_iota(jnp.int32, (4 * RANK, 4 * RANK), 0) // RANK
    col = lax.broadcasted_iota(jnp.int32, (4 * RANK, 4 * RANK), 1) // RANK
    lane = lax.broadcasted_iota(jnp.int32, (1, 4 * RANK), 1) // RANK
    for copy in copies:
        copy.wait()
    model_layer = slot_ref[lax.axis_index("lay") * lay_slots]

    for pair in range(pairs):
        block = query_ref[0, :, pair * 128:(pair + 1) * 128].astype(F32)
        rows_ref[pair * half:(pair + 1) * half, :] = jnp.where(slab == 0, block[:half], block[later:later + half])

    basis_ref[:RANK, :RANK] = out_ref[model_layer].astype(F32)
    out_rows = jnp.concatenate(
        [basis_ref[pl.ds(0, RANK // 2, stride=2), :], basis_ref[pl.ds(1, RANK // 2, stride=2), :]], axis=0
    )
    out_t = out_rows.T[:RANK].astype(BF16)
    out_rows = out_rows[:, :RANK].astype(BF16)
    out_twice = jnp.concatenate([out_rows, out_rows], axis=1)
    out_t_twice = jnp.concatenate([out_t, out_t], axis=1)

    in_wide = jnp.concatenate([in_ref[model_layer].astype(F32)] * 4, axis=1)
    in_tall = jnp.concatenate([in_wide] * 4, axis=0)
    in_diag = jnp.where(row == col, in_tall, F32(0.0)).astype(BF16)
    in_diag_t = jnp.where(row == col, in_tall.T, F32(0.0)).astype(BF16)
    eigen = jnp.concatenate([eigen_ref[model_layer]] * 4, axis=1)

    quads = range(half // 4)
    grids = []
    for quad in quads:
        tops, bottoms = [], []
        for two in range(2):
            at = quad * 4 + two * 2
            a = rows_ref[pl.ds(at, pairs, stride=half), :]
            b = rows_ref[pl.ds(at + 1, pairs, stride=half), :]
            tops.append(jnp.where(low_lanes, a, pltpu.roll(b, RANK, 1)))
            bottoms.append(jnp.where(low_lanes, pltpu.roll(a, RANK, 1), b))
        grids += [jnp.concatenate(tops, axis=1), jnp.concatenate(bottoms, axis=1)]
    right = jnp.dot(jnp.concatenate(grids, axis=0).astype(BF16), in_diag, preferred_element_type=F32)
    middles = [
        jnp.dot(
            out_t_twice, jnp.concatenate(split(right[quad * RANK:(quad + 1) * RANK]), axis=0),
            preferred_element_type=F32,
        )
        for quad in quads
    ]
    scaled = []
    for quad in quads:
        damp = jnp.zeros((1, 4 * RANK), F32)
        for one in range(4):
            block = block_ref[first + quad * 4 + one]
            value = F32(0.0)
            for k in range(BLOCKS):
                value = jnp.where(block == k, damping_ref[k], value)
            damp = jnp.where(lane == one, value, damp)
        scaled.append(middles[quad] / (eigen + damp))
    turned = [
        jnp.dot(out_twice, jnp.concatenate(split(block), axis=0), preferred_element_type=F32) for block in scaled
    ]
    hi, lo = split(jnp.concatenate(turned, axis=0))
    result = jnp.dot(hi, in_diag_t, preferred_element_type=F32)
    result = result + jnp.dot(lo, in_diag_t, preferred_element_type=F32)
    for quad in quads:
        for two in range(2):
            at = quad * 4 + two * 2
            top = result[quad * RANK:quad * RANK + pairs, two * 128:(two + 1) * 128]
            bottom = result[quad * RANK + pairs:(quad + 1) * RANK, two * 128:(two + 1) * 128]
            turned_ref[pl.ds(at, pairs, stride=half), :] = jnp.where(low_lanes, top, pltpu.roll(bottom, RANK, 1))
            turned_ref[pl.ds(at + 1, pairs, stride=half), :] = jnp.where(low_lanes, pltpu.roll(top, RANK, 1), bottom)

    for pair in range(pairs):
        result_ref[:, pair * 128:(pair + 1) * 128] = turned_ref[pair * half:(pair + 1) * half, :].astype(BF16)


def rotate(query_grads, query_block, layer_slot, out_basis, in_basis, eigen_values, damping):
    half = query_grads.shape[1] // lax.axis_size("slab")
    dim = query_grads.shape[2]
    operands = (query_grads, query_block, damping, layer_slot, out_basis, in_basis, eigen_values)
    span = -(-half // 16) * 16
    held = ((1, span, dim), *(x.shape for x in operands[1:]))
    homes = (pltpu.VMEM, pltpu.SMEM, pltpu.SMEM, pltpu.SMEM, pltpu.VMEM, pltpu.VMEM, pltpu.VMEM)
    return pl.pallas_call(
        functools.partial(rotate_kernel, half, 1),
        out_shape=jax.ShapeDtypeStruct((half, dim), BF16),
        in_specs=[pl.BlockSpec(memory_space=pltpu.HBM)] * len(operands),
        out_specs=pl.BlockSpec(memory_space=pltpu.VMEM),
        scratch_shapes=[home(shape, x.dtype) for home, shape, x in zip(homes, held, operands)] + [
            pltpu.VMEM((half * (dim // 128 + 1), 128), F32),
            pltpu.VMEM((RANK + 8, 128), F32),
            pltpu.VMEM((half * (dim // 128 + 1), 128), F32),
            pltpu.SemaphoreType.DMA((len(operands),)),
        ],
        compiler_params=pltpu.CompilerParams(vmem_limit_bytes=16 << 20),
        cost_estimate=pl.CostEstimate(flops=8 * half * dim * 256, bytes_accessed=1 << 20, transcendentals=0),
        name="rotate",
    )(*map(in_hbm, operands))


def fetch_kernel(shares, after_ref, store_hbm, store_ref, turned_ref, sems):
    del after_ref
    parts = sems.shape[0]
    rows = store_ref.shape[1] // parts
    copies = [
        pltpu.make_async_copy(
            store_hbm.at[:, pl.ds(k * rows, rows)], store_ref.at[:, pl.ds(k * rows, rows)], sems.at[k]
        )
        for k in range(parts)
    ]
    for copy in copies:
        copy.start()
    for copy in copies:
        copy.wait()
    lay = lax.axis_index("lay")
    for k in range(shares - 1):
        share = turned_ref.shape[2]
        owned = pl.ds(pl.multiple_of(lax.rem(lay + k + 1, shares) * share, share), share)
        turned_ref[k] = store_ref[0, owned, :].T


def fetch(after, store):
    shares = lax.axis_size("lay")
    _, examples, dim = store.shape
    vmem = pl.BlockSpec(memory_space=pltpu.VMEM)
    return pl.pallas_call(
        functools.partial(fetch_kernel, shares),
        out_shape=[
            jax.ShapeDtypeStruct(store.shape, store.dtype),
            jax.ShapeDtypeStruct((shares - 1, dim, examples // shares), store.dtype),
        ],
        in_specs=[vmem, pl.BlockSpec(memory_space=pltpu.HBM)],
        out_specs=[vmem] * 2,
        scratch_shapes=[pltpu.SemaphoreType.DMA((4,))],
        compiler_params=pltpu.CompilerParams(vmem_limit_bytes=24 << 20),
        cost_estimate=pl.CostEstimate(flops=0, bytes_accessed=2 * store.size * 2, transcendentals=0),
        name="fetch",
    )(after, in_hbm(store))


def score_kernel(count, height, share, shares, owners, turned, *refs):
    outs, held = refs[-1 - len(owners):-1], refs[-1]
    pieces, store_ref = refs[:-2 - len(owners)], refs[-2 - len(owners)]
    half = pieces[0].shape[0]
    for k, piece in enumerate(pieces[:count]):
        held[k * height:k * height + half, :] = piece[...]
    column = 0
    for piece in pieces[count:]:
        held[count * height:count * height + half, column:column + piece.shape[1]] = piece[...]
        column += piece.shape[1]
    lay = lax.axis_index("lay")
    for out, owner in zip(outs, owners):
        if not turned:
            rows = pl.ds(pl.multiple_of(lax.rem(lay + owner, shares) * share, share), share)
            block = lax.dot_general(held[...], store_ref[0, rows, :], NT, preferred_element_type=F32)
        else:
            block = jnp.dot(held[...], store_ref[owner - 1], preferred_element_type=F32)
        for j in range(out.shape[0] // half):
            out[j * half:(j + 1) * half, :] = block[j * height:j * height + half].astype(out.dtype)


def score(pieces, parts, store, owners, turned=False):
    half = (pieces + parts)[0].shape[0]
    dim = pieces[0].shape[1] if pieces else sum(part.shape[1] for part in parts)
    shares = lax.axis_size("lay")
    share = store.shape[2] if turned else store.shape[1] // shares
    whole = len(pieces) + (1 if parts else 0)
    height = -(-half // 16) * 16
    vmem = pl.BlockSpec(memory_space=pltpu.VMEM)
    return pl.pallas_call(
        functools.partial(score_kernel, len(pieces), height, share, shares, tuple(owners), turned),
        out_shape=[jax.ShapeDtypeStruct((whole * half, share), BF16 if owner else F32) for owner in owners],
        in_specs=[vmem] * (len(pieces) + len(parts) + 1),
        out_specs=[vmem] * len(owners),
        scratch_shapes=[pltpu.VMEM((whole * height, dim), BF16)],
        compiler_params=pltpu.CompilerParams(vmem_limit_bytes=24 << 20),
        cost_estimate=pl.CostEstimate(
            flops=2 * 256 * share * len(owners) * dim, bytes_accessed=1 << 20, transcendentals=0
        ),
        name="score",
    )(*pieces, *parts, store)


def swap_layers(sends):
    shares = lax.axis_size("lay")
    return [
        lax.ppermute(send, "lay", [(i, (i + k + 1) % shares) for i in range(shares)])
        for k, send in enumerate(sends)
    ]


def finish_kernel(half, members, sizes, first, rows_ref, sems, out_hbm, *refs):
    count = len(sizes)
    each = len(refs) // count
    slab, ex = lax.axis_index("slab"), lax.axis_index("ex")
    place = jnp.where(slab == 0, ex, 2 * members - 1 - ex)
    at, copies = first, []
    for k, size in enumerate(sizes):
        keep, got = refs[k * each], refs[k * each + 1:(k + 1) * each]
        for j in range(size):
            rows = slice(j * half, (j + 1) * half)
            total = keep[rows, :]
            for g in got:
                total = total + g[rows, :].astype(F32)
            distance = (at + 1) // 2
            hops = 2 * members - distance if at % 2 == 1 else distance
            source = lax.rem(place + hops, 2 * members)
            block = jnp.where(source < members, 2 * source, 2 * (2 * members - 1 - source) + 1)
            here = slice((at - first) * half, (at - first + 1) * half)
            rows_ref[here, :] = total
            copies.append(pltpu.make_async_copy(
                rows_ref.at[here, :], out_hbm.at[pl.ds(pl.multiple_of(block * half, 8), half), :], sems.at[at - first]
            ))
            copies[-1].start()
            at += 1
    for copy in copies:
        copy.wait()


def finish(half, sums, first=0, before=None):
    members = lax.axis_size("ex")
    vmem, hbm = pl.BlockSpec(memory_space=pltpu.VMEM), pl.BlockSpec(memory_space=pltpu.HBM)
    flat = [array for keep, got in sums for array in [keep, *got]]
    sizes = [keep.shape[0] // half for keep, _ in sums]
    share = flat[0].shape[1]
    ahead = [] if before is None else [before]

    def kernel(*refs):
        out_hbm, rows_ref, sems = refs[-3:]
        finish_kernel(half, members, sizes, first, rows_ref, sems, out_hbm, *refs[len(ahead):-3])

    return pl.pallas_call(
        kernel,
        out_shape=jax.ShapeDtypeStruct((2 * members * half, share), F32),
        in_specs=[hbm] * len(ahead) + [vmem] * len(flat),
        out_specs=hbm,
        input_output_aliases={0: 0} if ahead else {},
        scratch_shapes=[pltpu.VMEM((sum(sizes) * half, share), F32), pltpu.SemaphoreType.DMA((sum(sizes),))],
        compiler_params=pltpu.CompilerParams(vmem_limit_bytes=16 << 20),
        cost_estimate=pl.CostEstimate(flops=0, bytes_accessed=1 << 20, transcendentals=0),
        name="finish",
    )(*ahead, *flat)


def local(
    store_grads, query_grads, query_block, layer_slot, out_basis, in_basis, eigen_values, damping
):
    members = lax.axis_size("ex")
    ring = list(range(members)) + [members + i for i in reversed(range(members))]

    def hop(piece, steps):
        return lax.ppermute(piece, RING, [(a, ring[(i + steps) % len(ring)]) for i, a in enumerate(ring)])

    own = rotate(query_grads, query_block, layer_slot, out_basis, in_basis, eigen_values, damping)
    store, turned = fetch(own, store_grads)
    half, dim = own.shape
    others = range(1, lax.axis_size("lay"))
    one = two = own
    batch, sums = [own], []
    for step in range(1, members):
        if step == members - 1:
            cut = dim // 8 * 5 // 128 * 128
            parts = [one[:, :cut], two[:, cut:]]
        one, two = hop(one, 1), hop(two, -1)
        if step == members - 1:
            parts = [hop(parts[0], 2), hop(parts[1], -2)]
        if step == 1:
            one, store, turned = lax.optimization_barrier((one, store, turned))
        elif len(batch) >= 7:
            keep, *sends = score(batch, [], store, [0, *others])
            got = swap_layers(sends)
            if step < members - 1:
                one, _ = lax.optimization_barrier((one, sends))
            sums.append((keep, got))
            batch = []
        batch += [one, two]
    sends = score(batch, [], turned, others, True)
    near = swap_layers(sends)
    parts, _ = lax.optimization_barrier((parts, sends))
    far = swap_layers(score([], parts, turned, others, True))
    (keep,) = score(batch, parts, store, [0])
    rows = len(batch) * half
    sums.append((keep[:rows], near))
    scores = finish(half, sums)
    return finish(half, [(keep[rows:], far)], 2 * members - 1, scores).T


def solution(mesh):
    return jax.shard_map(
        local,
        mesh=mesh,
        in_specs=(
            P("lay", ("slab", "ex"), None),
            P("lay", ("pb", "ex"), None),
            P(),
            P(),
            P(),
            P(),
            P(),
            P(),
        ),
        out_specs=P(("slab", "ex", "lay"), "pb"),
        check_vma=False,
    )
```

```python
import functools

import jax
import jax.numpy as jnp
from jax import lax
from jax.experimental import pallas as pl
from jax.experimental.pallas import tpu as pltpu
from jax.sharding import PartitionSpec as P

RANK = 64
BLOCKS = 4
F32 = jnp.float32
BF16 = jnp.bfloat16
NT = (((1,), (1,)), ((), ()))
RING = ("slab", "ex")


def in_hbm(x):
    return pltpu.with_memory_space_constraint(x, pltpu.HBM)


def split(x):
    hi = x.astype(BF16)
    return hi, (x - hi.astype(F32)).astype(BF16)


def rotate_kernel(
    half, lay_slots, query_hbm, block_hbm, damping_hbm, slot_hbm, out_hbm, in_hbm, eigen_hbm,
    result_ref, query_ref, block_ref, damping_ref, slot_ref, out_ref, in_ref, eigen_ref,
    rows_ref, basis_ref, turned_ref, sems,
):
    pairs = RANK * RANK // 128
    local, span = query_hbm.shape[1], query_ref.shape[1]
    slab = lax.axis_index("slab")
    begin = pl.multiple_of(slab * (local - span), 16)
    later = half - (local - span)
    copies = [
        pltpu.make_async_copy(source, target, sems.at[k])
        for k, (source, target) in enumerate([
            (slot_hbm, slot_ref), (query_hbm.at[:, pl.ds(begin, span), :], query_ref), (block_hbm, block_ref), (damping_hbm, damping_ref),
            (out_hbm, out_ref), (in_hbm, in_ref), (eigen_hbm, eigen_ref),
        ])
    ]
    for copy in copies:
        copy.start()
    first = (lax.axis_index("pb") * lax.axis_size("ex") + lax.axis_index("ex")) * local + slab * half
    low_lanes = lax.broadcasted_iota(jnp.int32, (RANK // 2, 128), 1) < RANK
    row = lax.broadcasted_iota(jnp.int32, (4 * RANK, 4 * RANK), 0) // RANK
    col = lax.broadcasted_iota(jnp.int32, (4 * RANK, 4 * RANK), 1) // RANK
    lane = lax.broadcasted_iota(jnp.int32, (1, 4 * RANK), 1) // RANK
    for copy in copies:
        copy.wait()
    model_layer = slot_ref[lax.axis_index("lay") * lay_slots]

    for number, start in ((0, 0), (1, later)):
        @pl.when(slab == number)
        def _(start=start):
            for pair in range(pairs):
                block = query_ref[0, :, pair * 128:(pair + 1) * 128].astype(F32)
                rows_ref[pair * half:(pair + 1) * half, :] = block[start:start + half]

    basis_ref[:RANK, :RANK] = out_ref[model_layer].astype(F32)
    out_rows = jnp.concatenate(
        [basis_ref[pl.ds(0, RANK // 2, stride=2), :], basis_ref[pl.ds(1, RANK // 2, stride=2), :]], axis=0
    )
    out_t = out_rows.T[:RANK].astype(BF16)
    out_rows = out_rows[:, :RANK].astype(BF16)
    out_twice = jnp.concatenate([out_rows, out_rows], axis=1)
    out_t_twice = jnp.concatenate([out_t, out_t], axis=1)

    in_wide = jnp.concatenate([in_ref[model_layer].astype(F32)] * 4, axis=1)
    in_tall = jnp.concatenate([in_wide] * 4, axis=0)
    in_diag = jnp.where(row == col, in_tall, F32(0.0)).astype(BF16)
    in_diag_t = jnp.where(row == col, in_tall.T, F32(0.0)).astype(BF16)
    eigen = jnp.concatenate([eigen_ref[model_layer]] * 4, axis=1)

    quads = range(half // 4)
    grids = []
    for quad in quads:
        tops, bottoms = [], []
        for two in range(2):
            at = quad * 4 + two * 2
            a = rows_ref[pl.ds(at, pairs, stride=half), :]
            b = rows_ref[pl.ds(at + 1, pairs, stride=half), :]
            tops.append(jnp.where(low_lanes, a, pltpu.roll(b, RANK, 1)))
            bottoms.append(jnp.where(low_lanes, pltpu.roll(a, RANK, 1), b))
        grids += [jnp.concatenate(tops, axis=1), jnp.concatenate(bottoms, axis=1)]
    right = jnp.dot(jnp.concatenate(grids, axis=0).astype(BF16), in_diag, preferred_element_type=F32)
    middles = [
        jnp.dot(
            out_t_twice, jnp.concatenate(split(right[quad * RANK:(quad + 1) * RANK]), axis=0),
            preferred_element_type=F32,
        )
        for quad in quads
    ]
    scaled = []
    for quad in quads:
        damp = jnp.zeros((1, 4 * RANK), F32)
        for one in range(4):
            block = block_ref[first + quad * 4 + one]
            value = F32(0.0)
            for k in range(BLOCKS):
                value = jnp.where(block == k, damping_ref[k], value)
            damp = jnp.where(lane == one, value, damp)
        scaled.append(middles[quad] / (eigen + damp))
    turned = [
        jnp.dot(out_twice, jnp.concatenate(split(block), axis=0), preferred_element_type=F32) for block in scaled
    ]
    hi, lo = split(jnp.concatenate(turned, axis=0))
    result = jnp.dot(hi, in_diag_t, preferred_element_type=F32)
    result = result + jnp.dot(lo, in_diag_t, preferred_element_type=F32)
    for quad in quads:
        for two in range(2):
            at = quad * 4 + two * 2
            top = result[quad * RANK:quad * RANK + pairs, two * 128:(two + 1) * 128]
            bottom = result[quad * RANK + pairs:(quad + 1) * RANK, two * 128:(two + 1) * 128]
            turned_ref[pl.ds(at, pairs, stride=half), :] = jnp.where(low_lanes, top, pltpu.roll(bottom, RANK, 1))
            turned_ref[pl.ds(at + 1, pairs, stride=half), :] = jnp.where(low_lanes, pltpu.roll(top, RANK, 1), bottom)

    for pair in range(pairs):
        result_ref[:, pair * 128:(pair + 1) * 128] = turned_ref[pair * half:(pair + 1) * half, :].astype(BF16)


def rotate(query_grads, query_block, layer_slot, out_basis, in_basis, eigen_values, damping):
    half = query_grads.shape[1] // lax.axis_size("slab")
    dim = query_grads.shape[2]
    operands = (query_grads, query_block, damping, layer_slot, out_basis, in_basis, eigen_values)
    span = -(-half // 16) * 16
    held = ((1, span, dim), *(x.shape for x in operands[1:]))
    homes = (pltpu.VMEM, pltpu.SMEM, pltpu.SMEM, pltpu.SMEM, pltpu.VMEM, pltpu.VMEM, pltpu.VMEM)
    return pl.pallas_call(
        functools.partial(rotate_kernel, half, 1),
        out_shape=jax.ShapeDtypeStruct((half, dim), BF16),
        in_specs=[pl.BlockSpec(memory_space=pltpu.HBM)] * len(operands),
        out_specs=pl.BlockSpec(memory_space=pltpu.VMEM),
        scratch_shapes=[home(shape, x.dtype) for home, shape, x in zip(homes, held, operands)] + [
            pltpu.VMEM((half * (dim // 128 + 1), 128), F32),
            pltpu.VMEM((RANK + 8, 128), F32),
            pltpu.VMEM((half * (dim // 128 + 1), 128), F32),
            pltpu.SemaphoreType.DMA((len(operands),)),
        ],
        compiler_params=pltpu.CompilerParams(vmem_limit_bytes=16 << 20),
        cost_estimate=pl.CostEstimate(flops=8 * half * dim * 256, bytes_accessed=1 << 20, transcendentals=0),
        name="rotate",
    )(*map(in_hbm, operands))


def fetch_kernel(shares, after_ref, store_hbm, store_ref, turned_ref, sems):
    del after_ref
    parts = sems.shape[0]
    rows = store_ref.shape[1] // parts
    copies = [
        pltpu.make_async_copy(
            store_hbm.at[:, pl.ds(k * rows, rows)], store_ref.at[:, pl.ds(k * rows, rows)], sems.at[k]
        )
        for k in range(parts)
    ]
    for copy in copies:
        copy.start()
    for copy in copies:
        copy.wait()
    lay = lax.axis_index("lay")
    for k in range(shares - 1):
        share = turned_ref.shape[2]
        owned = pl.ds(pl.multiple_of(lax.rem(lay + k + 1, shares) * share, share), share)
        turned_ref[k] = store_ref[0, owned, :].T


def fetch(after, store):
    shares = lax.axis_size("lay")
    _, examples, dim = store.shape
    vmem = pl.BlockSpec(memory_space=pltpu.VMEM)
    return pl.pallas_call(
        functools.partial(fetch_kernel, shares),
        out_shape=[
            jax.ShapeDtypeStruct(store.shape, store.dtype),
            jax.ShapeDtypeStruct((shares - 1, dim, examples // shares), store.dtype),
        ],
        in_specs=[vmem, pl.BlockSpec(memory_space=pltpu.HBM)],
        out_specs=[vmem] * 2,
        scratch_shapes=[pltpu.SemaphoreType.DMA((4,))],
        compiler_params=pltpu.CompilerParams(vmem_limit_bytes=24 << 20),
        cost_estimate=pl.CostEstimate(flops=0, bytes_accessed=2 * store.size * 2, transcendentals=0),
        name="fetch",
    )(after, in_hbm(store))


def score_kernel(count, height, share, shares, owners, turned, *refs):
    outs, held = refs[-1 - len(owners):-1], refs[-1]
    pieces, store_ref = refs[:-2 - len(owners)], refs[-2 - len(owners)]
    half = pieces[0].shape[0]
    for k, piece in enumerate(pieces[:count]):
        held[k * height:k * height + half, :] = piece[...]
    column = 0
    for piece in pieces[count:]:
        held[count * height:count * height + half, column:column + piece.shape[1]] = piece[...]
        column += piece.shape[1]
    lay = lax.axis_index("lay")
    for out, owner in zip(outs, owners):
        if not turned:
            rows = pl.ds(pl.multiple_of(lax.rem(lay + owner, shares) * share, share), share)
            block = lax.dot_general(held[...], store_ref[0, rows, :], NT, preferred_element_type=F32)
        else:
            block = jnp.dot(held[...], store_ref[owner - 1], preferred_element_type=F32)
        for j in range(out.shape[0] // half):
            out[j * half:(j + 1) * half, :] = block[j * height:j * height + half].astype(out.dtype)


def score(pieces, parts, store, owners, turned=False):
    half = (pieces + parts)[0].shape[0]
    dim = pieces[0].shape[1] if pieces else sum(part.shape[1] for part in parts)
    shares = lax.axis_size("lay")
    share = store.shape[2] if turned else store.shape[1] // shares
    whole = len(pieces) + (1 if parts else 0)
    height = -(-half // 16) * 16
    vmem = pl.BlockSpec(memory_space=pltpu.VMEM)
    return pl.pallas_call(
        functools.partial(score_kernel, len(pieces), height, share, shares, tuple(owners), turned),
        out_shape=[jax.ShapeDtypeStruct((whole * half, share), BF16 if owner else F32) for owner in owners],
        in_specs=[vmem] * (len(pieces) + len(parts) + 1),
        out_specs=[vmem] * len(owners),
        scratch_shapes=[pltpu.VMEM((whole * height, dim), BF16)],
        compiler_params=pltpu.CompilerParams(vmem_limit_bytes=24 << 20),
        cost_estimate=pl.CostEstimate(
            flops=2 * 256 * share * len(owners) * dim, bytes_accessed=1 << 20, transcendentals=0
        ),
        name="score",
    )(*pieces, *parts, store)


def swap_layers(sends):
    shares = lax.axis_size("lay")
    return [
        lax.ppermute(send, "lay", [(i, (i + k + 1) % shares) for i in range(shares)])
        for k, send in enumerate(sends)
    ]


def finish_kernel(half, members, sizes, first, rows_ref, sems, out_hbm, *refs):
    count = len(sizes)
    each = len(refs) // count
    slab, ex = lax.axis_index("slab"), lax.axis_index("ex")
    place = jnp.where(slab == 0, ex, 2 * members - 1 - ex)
    at, copies = first, []
    for k, size in enumerate(sizes):
        keep, got = refs[k * each], refs[k * each + 1:(k + 1) * each]
        for j in range(size):
            rows = slice(j * half, (j + 1) * half)
            total = keep[rows, :]
            for g in got:
                total = total + g[rows, :].astype(F32)
            distance = (at + 1) // 2
            hops = 2 * members - distance if at % 2 == 1 else distance
            source = lax.rem(place + hops, 2 * members)
            block = jnp.where(source < members, 2 * source, 2 * (2 * members - 1 - source) + 1)
            here = slice((at - first) * half, (at - first + 1) * half)
            rows_ref[here, :] = total
            copies.append(pltpu.make_async_copy(
                rows_ref.at[here, :], out_hbm.at[pl.ds(pl.multiple_of(block * half, 8), half), :], sems.at[at - first]
            ))
            copies[-1].start()
            at += 1
    for copy in copies:
        copy.wait()


def finish(half, sums, first=0, before=None):
    members = lax.axis_size("ex")
    vmem, hbm = pl.BlockSpec(memory_space=pltpu.VMEM), pl.BlockSpec(memory_space=pltpu.HBM)
    flat = [array for keep, got in sums for array in [keep, *got]]
    sizes = [keep.shape[0] // half for keep, _ in sums]
    share = flat[0].shape[1]
    ahead = [] if before is None else [before]

    def kernel(*refs):
        out_hbm, rows_ref, sems = refs[-3:]
        finish_kernel(half, members, sizes, first, rows_ref, sems, out_hbm, *refs[len(ahead):-3])

    return pl.pallas_call(
        kernel,
        out_shape=jax.ShapeDtypeStruct((2 * members * half, share), F32),
        in_specs=[hbm] * len(ahead) + [vmem] * len(flat),
        out_specs=hbm,
        input_output_aliases={0: 0} if ahead else {},
        scratch_shapes=[pltpu.VMEM((sum(sizes) * half, share), F32), pltpu.SemaphoreType.DMA((sum(sizes),))],
        compiler_params=pltpu.CompilerParams(vmem_limit_bytes=16 << 20),
        cost_estimate=pl.CostEstimate(flops=0, bytes_accessed=1 << 20, transcendentals=0),
        name="finish",
    )(*ahead, *flat)


def local(
    store_grads, query_grads, query_block, layer_slot, out_basis, in_basis, eigen_values, damping
):
    members = lax.axis_size("ex")
    ring = list(range(members)) + [members + i for i in reversed(range(members))]

    def hop(piece, steps):
        return lax.ppermute(piece, RING, [(a, ring[(i + steps) % len(ring)]) for i, a in enumerate(ring)])

    own = rotate(query_grads, query_block, layer_slot, out_basis, in_basis, eigen_values, damping)
    store, turned = fetch(own, store_grads)
    half, dim = own.shape
    others = range(1, lax.axis_size("lay"))
    one = two = own
    batch, sums = [own], []
    for step in range(1, members):
        if step == members - 1:
            cut = dim // 8 * 5 // 128 * 128
            parts = [one[:, :cut], two[:, cut:]]
        one, two = hop(one, 1), hop(two, -1)
        if step == members - 1:
            parts = [hop(parts[0], 2), hop(parts[1], -2)]
        if step == 1:
            one, store, turned = lax.optimization_barrier((one, store, turned))
        elif len(batch) >= 7:
            keep, *sends = score(batch, [], store, [0, *others])
            got = swap_layers(sends)
            if step < members - 1:
                one, _ = lax.optimization_barrier((one, sends))
            sums.append((keep, got))
            batch = []
        batch += [one, two]
    sends = score(batch, [], turned, others, True)
    near = swap_layers(sends)
    parts, _ = lax.optimization_barrier((parts, sends))
    far = swap_layers(score([], parts, turned, others, True))
    (keep,) = score(batch, parts, store, [0])
    rows = len(batch) * half
    sums.append((keep[:rows], near))
    scores = finish(half, sums)
    return finish(half, [(keep[rows:], far)], 2 * members - 1, scores).T


def solution(mesh):
    return jax.shard_map(
        local,
        mesh=mesh,
        in_specs=(
            P("lay", ("slab", "ex"), None),
            P("lay", ("pb", "ex"), None),
            P(),
            P(),
            P(),
            P(),
            P(),
            P(),
        ),
        out_specs=P(("slab", "ex", "lay"), "pb"),
        check_vma=False,
    )
```
